32 devices in a mesh: slab: 2 (over x), tile: 4 (over y, core), view: 4 (over z).
Axes of the slice: x: 2, y: 2, z: 4, core: 2. Of those that a mesh axis runs over, the one named last changes fastest.
Arguments:
- estimate: float32 [32, 256, 128], P('slab', 'tile'), may hold values from 0.25 to 4
- measured: float32 [4, 32, 256, 128], P('view', 'slab', 'tile'), may hold values from 0.25 to 4
- psf_taps: float32 [4, 3, 31], P('view'), may hold values from 0.3 to 1
- plane_source: int32 [4, 32], P('view'), may hold values from 0 to 31, as said below
- plane_shift: int32 [4, 32], P('view'), may hold values from 0 to 127
Outputs:
- new_estimate: float32 [32, 256, 128], P('slab', 'tile', 'view')
The draws below stay inside these ranges and needn't reach their ends.
Inputs may be any that keep to these rules, and one draw needn't show every extreme that they name: `plane_source`: for each view, the 16 camera planes of one aligned block of 16 take their sample planes from 2 different aligned blocks of 16 sample planes, exactly 8 from each; a sample plane may be shown several times or not at all.
All inputs are finite; a program needn't handle non-finite values.
Results may differ from the reference program's by a relative error of at most 0.0001.
Values sent between devices are 32-bit elements; how exact they have to be, the bound alone decides.
No kernel may reach another device: no remote copies, remote signals or barrier semaphores. Data moves between devices by JAX's collectives and lax.ppermute only.
A program may use at most 64 MiB of HBM per device.

```python
import math
import jax
import jax.numpy as jnp
from jax import lax

ZD = 16
X = 128
TAPS = 31
VIEWS = 4
Z = 32
Y = 256
CAP = 8


def draw_plane_source(key, part):
    stride_key, within_key = jax.random.split(jax.random.fold_in(key, 7))
    devices = Z // ZD
    strides = jax.random.randint(stride_key, (VIEWS, 1, 1), 1, max(devices, 2))
    camera = jnp.broadcast_to(jnp.arange(devices, dtype=jnp.int32)[None, :, None], (VIEWS, devices, ZD))
    slot_index = jnp.broadcast_to(jnp.arange(ZD, dtype=jnp.int32)[None, None, :], (VIEWS, devices, ZD))
    owners = jnp.mod(camera * strides + slot_index // CAP, devices)
    within = jax.random.randint(within_key, (VIEWS, devices, ZD), 0, ZD)
    return (owners * ZD + within).reshape(VIEWS, Z).astype(jnp.int32)


def touch_ends(result, own_key, least, high):
    spot = [jax.random.randint(jax.random.fold_in(own_key, axis), (), 0, length) for axis, length in enumerate(result.shape)]
    widest = result.shape.index(max(result.shape))
    next_to = spot[:widest] + [(spot[widest] + 1) % result.shape[widest]] + spot[widest + 1:]
    return result.at[tuple(spot)].set(least).at[tuple(next_to)].set(high)


def shard_levels(key, extent, cuts, least, high):
    factor_of, own = 1.0, jax.random.fold_in(key, 6)
    for position, parts in cuts:
        draws = jnp.exp(jax.random.uniform(jax.random.fold_in(own, position), (parts,), jnp.float32, least / len(cuts), high / len(cuts)))
        factor_of = factor_of * jnp.repeat(draws, extent[position] // parts).reshape([-1 if axis == position else 1 for axis in range(len(extent))])
    return factor_of


def setup_inputs(seed: int = 0) -> dict:
    key_list = jax.random.split(jax.random.key(seed), 6)
    return {
        "estimate": jnp.clip(jnp.exp(math.log(4.0) - 2.7725887 * jax.random.uniform(key_list[0], (Z, Y, X), jnp.float32) ** shard_levels(key_list[0], (Z, Y, X), ((0, 2), (1, 4)), -0.2, 0.2)), 0.25, 4.0),
        "measured": jnp.clip(jnp.exp(math.log(4.0) - 2.7725887 * jax.random.uniform(key_list[1], (VIEWS, Z, Y, X), jnp.float32) ** shard_levels(key_list[1], (VIEWS, Z, Y, X), ((0, 4), (1, 2), (2, 4)), -0.2, 0.2)), 0.25, 4.0),
        "psf_taps": jnp.clip(jnp.exp(math.log(1.0) - 1.2039728 * jax.random.uniform(key_list[2], (VIEWS, 3, TAPS), jnp.float32) ** shard_levels(key_list[2], (VIEWS, 3, TAPS), ((0, 4),), -0.2, 0.2)), 0.3, 1.0),
        "plane_source": draw_plane_source(jax.random.fold_in(key_list[5], 71), 0),
        "plane_shift": touch_ends(jax.random.randint(key_list[4], (VIEWS, Z), 0, X), jax.random.fold_in(key_list[4], 1), 0, X - 1).astype(jnp.int32),
    }


def cyclic_blur(volume, kernel, axis, direction):
    radius = (kernel.shape[0] - 1) // 2
    summed = jnp.zeros_like(volume)
    for tap_index in range(kernel.shape[0]):
        summed = summed + kernel[tap_index] * jnp.roll(volume, direction * (radius - tap_index), axis=axis)
    return summed


def reference(estimate, measured, psf_taps, plane_source, plane_shift):
    kernels = psf_taps / jnp.sum(psf_taps, axis=2, keepdims=True)
    x_width = estimate.shape[2]
    col_index = lax.broadcasted_iota(jnp.int32, (1, 1, x_width), 2)
    summed = jnp.zeros_like(estimate)
    for view_index in range(VIEWS):
        blurred = cyclic_blur(estimate, kernels[view_index, 0], 0, 1)
        blurred = cyclic_blur(blurred, kernels[view_index, 1], 1, 1)
        blurred = cyclic_blur(blurred, kernels[view_index, 2], 2, 1)
        sources = plane_source[view_index].astype(jnp.int32)
        shifts = plane_shift[view_index].astype(jnp.int32)
        camera = jnp.take(blurred, sources, axis=0)
        x_index = jnp.mod(col_index - shifts[:, None, None], x_width).astype(jnp.int32)
        forward = jnp.take_along_axis(camera, jnp.broadcast_to(x_index, camera.shape), axis=2)
        ratio_planes = measured[view_index] / forward
        back_index = jnp.mod(col_index + shifts[:, None, None], x_width).astype(jnp.int32)
        unsheared = jnp.take_along_axis(ratio_planes, jnp.broadcast_to(back_index, camera.shape), axis=2)
        pulled = jax.ops.segment_sum(unsheared, sources, num_segments=estimate.shape[0])
        correction = cyclic_blur(pulled, kernels[view_index, 2], 2, -1)
        correction = cyclic_blur(correction, kernels[view_index, 1], 1, -1)
        correction = cyclic_blur(correction, kernels[view_index, 0], 0, -1)
        summed = summed + correction
    return estimate * summed / VIEWS
```

```python
import functools

import jax
import jax.numpy as jnp
from jax import lax
from jax.experimental import pallas as pl
from jax.experimental.pallas import tpu as pltpu
from jax.sharding import PartitionSpec as P

F32 = jnp.float32
BF16 = jnp.bfloat16
HALO = 16
VMEM_LIMIT = 40 * 1024 * 1024


def split(x):
    high = x.astype(BF16)
    low = (x - high.astype(F32)).astype(BF16)
    return high, low


def dot(a, b):
    return jnp.dot(a, b, preferred_element_type=F32)


def iota(shape, axis):
    return lax.broadcasted_iota(jnp.int32, shape, axis)


def by_taps(offset, taps_ref, axis, inside=None):
    taps = taps_ref.shape[1]
    out = jnp.zeros(offset.shape, F32)
    for t in range(taps):
        out = jnp.where(offset == t, taps_ref[axis, t], out)
    return out if inside is None else jnp.where(inside, out, 0.0)


def left_pack(full):
    high, low = split(full)
    return jnp.concatenate(
        [jnp.concatenate([high, high], 1), jnp.concatenate([low, jnp.zeros_like(low)], 1)], 0
    )


def right_pack(full):
    high, low = split(full)
    return jnp.concatenate(
        [jnp.concatenate([high, low], 1), jnp.concatenate([high, jnp.zeros_like(low)], 1)], 0
    )


def prepare_kernel(geometry, taps_ref, sources_ref, place_ref, wf_ref, wb_ref, yf_ref, yb_ref, xf_ref, xb_ref):
    devices, planes, rows, width, views = geometry
    depth = devices * planes
    own = place_ref[0]
    radius = (taps_ref.shape[1] - 1) // 2
    cells = planes * 8
    row = iota((cells, cells), 0)
    col = iota((cells, cells), 1)
    diagonal = (row & 7) == (col & 7)
    source_row = jnp.zeros((cells, cells), jnp.int32)
    source_col = jnp.zeros((cells, cells), jnp.int32)
    for p in range(planes):
        source = sources_ref[own * planes + p]
        source_row = jnp.where((row >> 3) == p, source, source_row)
        source_col = jnp.where((col >> 3) == p, source, source_col)

    def block(d, carry):
        slab = lax.rem(own - d + devices, devices)
        offset = slab * planes + (col >> 3) - source_row + radius
        offset = jnp.where(offset < 0, offset + depth, offset)
        offset = jnp.where(offset >= depth, offset - depth, offset)
        wf_ref[d] = left_pack(by_taps(offset, taps_ref, 0, diagonal))
        offset = slab * planes + (row >> 3) - source_col + radius
        offset = jnp.where(offset < 0, offset + depth, offset)
        offset = jnp.where(offset >= depth, offset - depth, offset)
        wb_ref[d] = left_pack(by_taps(offset, taps_ref, 0, diagonal))
        return carry

    lax.fori_loop(0, devices, block, 0)

    extended = rows + 2 * HALO
    row = iota((rows, 2 * extended), 0)
    col = iota((rows, 2 * extended), 1)
    first = col < extended
    col = jnp.where(first, col, col - extended)
    for ref, offset in (
        (yf_ref, col - row - (HALO - radius)),
        (yb_ref, row - col + (HALO + radius)),
    ):
        full = by_taps(offset, taps_ref, 1)
        high = full.astype(BF16)
        low = jnp.where(first, full - high.astype(F32), 0.0).astype(BF16)
        ref[...] = jnp.concatenate([high, low], 0)

    row = iota((width, width), 0)
    col = iota((width, width), 1)
    offset = row - col + radius
    offset = jnp.where(offset < 0, offset + width, offset)
    offset = jnp.where(offset >= width, offset - width, offset)
    xf_ref[...] = right_pack(by_taps(offset, taps_ref, 2))
    offset = col - row + radius
    offset = jnp.where(offset < 0, offset + width, offset)
    offset = jnp.where(offset >= width, offset - width, offset)
    back = by_taps(offset, taps_ref, 2)
    for j in range(views):
        xb_ref[j] = right_pack(pltpu.roll(back, j * (width // views), 1) if j else back)


def mix_kernel(blocks, *refs):
    slab_refs, wf_ref, cam_ref, top_ref, bottom_ref = refs[:blocks], *refs[blocks:]
    planes, rows, width = cam_ref.shape
    cells = planes * 8
    for start in range(0, rows, 16):
        total = None
        for d in range(blocks):
            cell = jnp.concatenate(
                [slab_refs[d][:, start + s : start + s + 8, :].reshape(cells, width) for s in (0, 8)], 1
            )
            part = dot(wf_ref[d], jnp.concatenate(split(cell), 0))
            total = part if total is None else total + part
        total = total[:cells] + total[cells:]
        for s in (0, 8):
            piece = total[:, (s // 8) * width : (s // 8 + 1) * width].reshape(planes, 8, width)
            cam_ref[:, start + s : start + s + 8, :] = piece
            if start < HALO:
                top_ref[:, start + s : start + s + 8, :] = piece
            if start >= rows - HALO:
                at = start + s - (rows - HALO)
                bottom_ref[:, at : at + 8, :] = piece


def blur_row_pair(p, band, above_ref, mid_ref, below_ref):
    rows = mid_ref.shape[1]
    pair = jnp.concatenate(
        [jnp.concatenate([above_ref[q], mid_ref[q], below_ref[q]], 0) for q in (p, p + 1)], 1
    )
    out = dot(band, jnp.concatenate(split(pair), 0))
    return out[:rows] + out[rows:]


def ratio_kernel(
    shifts_ref, place_ref, cam_ref, above_ref, below_ref, measured_ref, yf_ref, xf_ref, out_ref, top_ref, bottom_ref
):
    planes, rows, width = cam_ref.shape
    base = place_ref[0] * planes
    band = yf_ref[...]
    circle = xf_ref[...]
    for p in range(0, planes, 2):
        pair = blur_row_pair(p, band, above_ref, cam_ref, below_ref)
        pair = jnp.concatenate([pair[:, :width], pair[:, width:]], 0)
        pair = dot(jnp.concatenate(split(pair), 1), circle)
        pair = pair[:, :width] + pair[:, width:]
        for q in (0, 1):
            shift = shifts_ref[base + p + q]
            forward = pltpu.roll(pair[q * rows : (q + 1) * rows], shift, 1)
            ratio = measured_ref[0, p + q] / forward
            back = lax.rem(width - shift, width)
            ratio = pltpu.roll(ratio, back, 1)
            out_ref[p + q] = ratio
            top_ref[p + q] = ratio[:HALO]
            bottom_ref[p + q] = ratio[rows - HALO :]


def pull_kernel(blocks, ratio_ref, above_ref, below_ref, yb_ref, wb_ref, *refs):
    out_refs, rows_ref = refs[:blocks], refs[blocks]
    planes, rows, width = ratio_ref.shape
    cells = planes * 8
    band = yb_ref[...]
    for p in range(0, planes, 2):
        pair = blur_row_pair(p, band, above_ref, ratio_ref, below_ref)
        rows_ref[p] = pair[:, :width]
        rows_ref[p + 1] = pair[:, width:]
    for start in range(0, rows, 16):
        cell = jnp.concatenate(
            [rows_ref[:, start + s : start + s + 8, :].reshape(cells, width) for s in (0, 8)], 1
        )
        cell = jnp.concatenate(split(cell), 0)
        for d in range(blocks):
            part = dot(wb_ref[d], cell)
            part = part[:cells] + part[cells:]
            for s in (0, 8):
                out_refs[d][:, start + s : start + s + 8, :] = part[
                    :, (s // 8) * width : (s // 8 + 1) * width
                ].reshape(planes, 8, width)


def share_kernel(blocks, views, place_ref, *refs):
    slab_refs, xb_ref, out_refs = refs[:blocks], refs[blocks], refs[blocks + 1 :]
    planes, rows, width = slab_refs[0].shape
    group = planes // views
    own = place_ref[1]
    share = width // views
    lane_block = iota((group * rows, width), 1) // share
    results = []
    for j in range(views):
        total = slab_refs[0][j * group : (j + 1) * group]
        for ref in slab_refs[1:]:
            total = total + ref[j * group : (j + 1) * group]
        out = dot(jnp.concatenate(split(total.reshape(group * rows, width)), 1), xb_ref[j])
        results.append(out[:, :width] + out[:, width:])
    for k in range(views):
        packed = results[0]
        for j in range(1, views):
            packed = jnp.where(lane_block == lax.rem(own + k + j, views), results[j], packed)
        out_refs[k][...] = packed


def update_kernel(views, place_ref, estimate_ref, *refs):
    share_refs, out_ref = refs[:views], refs[views]
    planes, rows, width = estimate_ref.shape
    group = planes // views
    share = width // views
    own = place_ref[1]
    total = share_refs[0][...]
    for ref in share_refs[1:]:
        total = total + ref[...]
    total = total * (1.0 / views)
    for j in range(views):
        block = lax.rem(own + j, views)
        mine = pltpu.roll(total, lax.rem(width - block * share, width), 1)
        old = estimate_ref[j * group : (j + 1) * group].reshape(group * rows, width)
        old = pltpu.roll(old, lax.rem(width - own * share, width), 1)
        out_ref[j * group : (j + 1) * group] = (mine * old)[:, :share].reshape(group, rows, share)


def call(kernel, outs, specs, flops, name, scratch=()):
    smem = pl.BlockSpec(memory_space=pltpu.SMEM)
    vmem = pl.BlockSpec(memory_space=pltpu.VMEM)
    single = not isinstance(outs, (list, tuple))
    return pl.pallas_call(
        kernel,
        out_shape=outs,
        in_specs=[smem if s == "s" else vmem for s in specs],
        out_specs=vmem if single else [vmem] * len(outs),
        scratch_shapes=list(scratch),
        compiler_params=pltpu.CompilerParams(vmem_limit_bytes=VMEM_LIMIT),
        cost_estimate=pl.CostEstimate(flops=flops, bytes_accessed=2 << 20, transcendentals=0),
        name=name,
    )


def local(estimate, measured, psf_taps, plane_source, plane_shift):
    planes, rows, width = estimate.shape
    devices = lax.axis_size("slab")
    tiles = lax.axis_size("tile")
    views = lax.axis_size("view")
    slab = lax.axis_index("slab")
    view = lax.axis_index("view")
    cells = planes * 8
    whole = jax.ShapeDtypeStruct((planes, rows, width), F32)
    edge = jax.ShapeDtypeStruct((planes, HALO, width), F32)

    def matrix(*shape):
        return jax.ShapeDtypeStruct(shape, BF16)

    def exchange_rows(top, bottom):
        above = lax.ppermute(bottom, "tile", [(i, (i + 1) % tiles) for i in range(tiles)])
        below = lax.ppermute(top, "tile", [((i + 1) % tiles, i) for i in range(tiles)])
        return above, below

    slabs = [estimate] + [
        lax.ppermute(estimate, "slab", [(i, (i + d) % devices) for i in range(devices)])
        for d in range(1, devices)
    ]
    kernels = psf_taps[0] / jnp.sum(psf_taps[0], axis=1, keepdims=True)
    place = jnp.stack([slab, view]).astype(jnp.int32)
    wf, wb, yf, yb, xf, xb = call(
        functools.partial(prepare_kernel, (devices, planes, rows, width, views)),
        [
            matrix(devices, 2 * cells, 2 * cells),
            matrix(devices, 2 * cells, 2 * cells),
            matrix(2 * rows, 2 * (rows + 2 * HALO)),
            matrix(2 * rows, 2 * (rows + 2 * HALO)),
            matrix(2 * width, 2 * width),
            matrix(views, 2 * width, 2 * width),
        ],
        "sss",
        1 << 24,
        "prepare",
    )(kernels, plane_source[0], place)

    camera, top, bottom = call(
        functools.partial(mix_kernel, devices), [whole, edge, edge], "v" * (devices + 1), 1 << 28, "mix"
    )(*slabs, wf)
    above, below = exchange_rows(top, bottom)
    ratio, top, bottom = call(ratio_kernel, [whole, edge, edge], "ssvvvvvv", 1 << 28, "ratio")(
        plane_shift[0], place, camera, above, below, measured, yf, xf
    )
    above, below = exchange_rows(top, bottom)
    parts = call(
        functools.partial(pull_kernel, devices),
        [whole] * devices,
        "vvvvv",
        1 << 28,
        "pull",
        [pltpu.VMEM((planes, rows, width), F32)],
    )(ratio, above, below, yb, wb)
    received = [parts[0]] + [
        lax.ppermute(parts[d], "slab", [(i, (i - d) % devices) for i in range(devices)])
        for d in range(1, devices)
    ]
    shares = call(
        functools.partial(share_kernel, devices, views),
        [jax.ShapeDtypeStruct((planes // views * rows, width), F32)] * views,
        "s" + "v" * (devices + 1),
        1 << 28,
        "share",
    )(place, *received, xb)
    shares = [shares[0]] + [
        lax.ppermute(shares[k], "view", [(i, (i + k) % views) for i in range(views)]) for k in range(1, views)
    ]
    return call(
        functools.partial(update_kernel, views),
        jax.ShapeDtypeStruct((planes, rows, width // views), F32),
        "sv" + "v" * views,
        1 << 24,
        "update",
    )(place, estimate, *shares)


def solution(mesh):
    in_specs = (
        P("slab", "tile", None),
        P("view", "slab", "tile", None),
        P("view", None, None),
        P("view", None),
        P("view", None),
    )
    out_specs = P("slab", "tile", "view")
    return jax.shard_map(local, mesh=mesh, in_specs=in_specs, out_specs=out_specs, check_vma=False)
```

```python
import functools

import jax
import jax.numpy as jnp
from jax import lax
from jax.experimental import pallas as pl
from jax.experimental.pallas import tpu as pltpu
from jax.sharding import PartitionSpec as P

F32 = jnp.float32
BF16 = jnp.bfloat16
HALO = 16
LANES = 128
VMEM_LIMIT = 40 * 1024 * 1024


def split(x, axis):
    high = x.astype(BF16)
    low = (x - high.astype(F32)).astype(BF16)
    return jnp.concatenate([high, low], axis)


def dot(a, b, b_axis=0):
    return lax.dot_general(a, b, (((1,), (b_axis,)), ((), ())), preferred_element_type=F32)


def halves(x, axis):
    middle = x.shape[axis] // 2
    return lax.slice_in_dim(x, 0, middle, axis=axis) + lax.slice_in_dim(x, middle, 2 * middle, axis=axis)


def iota(shape, axis):
    return lax.broadcasted_iota(jnp.int32, shape, axis)


def wrapped(offset, length):
    offset = jnp.where(offset < 0, offset + length, offset)
    return jnp.where(offset >= length, offset - length, offset)


def by_taps(offset, taps_ref, axis):
    out = jnp.zeros(offset.shape, F32)
    for t in range(taps_ref.shape[1]):
        out = jnp.where(offset == t, taps_ref[axis, t], out)
    return out


def left_pack(full):
    high = full.astype(BF16)
    low = (full - high.astype(F32)).astype(BF16)
    return jnp.concatenate(
        [jnp.concatenate([high, high], 1), jnp.concatenate([low, jnp.zeros_like(low)], 1)], 0
    )


def right_pack(full):
    high = full.astype(BF16)
    low = (full - high.astype(F32)).astype(BF16)
    return jnp.concatenate(
        [jnp.concatenate([high, low], 1), jnp.concatenate([high, jnp.zeros_like(low)], 1)], 0
    )


def row_band(taps_ref, out_rows, in_rows, lead, back):
    row = iota((out_rows, 2 * in_rows), 0)
    col = iota((out_rows, 2 * in_rows), 1)
    first = col < in_rows
    col = jnp.where(first, col, col - in_rows)
    full = by_taps(row - col + lead if back else col - row - lead, taps_ref, 1)
    high = full.astype(BF16)
    low = jnp.where(first, full - high.astype(F32), 0.0).astype(BF16)
    return jnp.concatenate([high, low], 0)


def prepare_kernel(
    devices, views, taps_ref, meta_ref, edge_ref, inner_ref,
    wf_ref, wb_ref, yf_ref, yi_ref, ye_ref, xf_ref, xb_ref, old_edge_ref, old_inner_ref, turned_ref,
):
    planes, inner, width = inner_ref.shape
    rows = inner + 2 * HALO
    depth = devices * planes
    own, view = meta_ref[0], meta_ref[1]
    radius = (taps_ref.shape[1] - 1) // 2
    cells = planes * 8
    row = iota((cells, cells), 0)
    col = iota((cells, cells), 1)
    diagonal = (row & 7) == (col & 7)
    source_row = jnp.zeros((cells, cells), jnp.int32)
    source_col = jnp.zeros((cells, cells), jnp.int32)
    for p in range(planes):
        source = meta_ref[2 + own * planes + p]
        source_row = jnp.where((row >> 3) == p, source, source_row)
        source_col = jnp.where((col >> 3) == p, source, source_col)

    def block(d, carry):
        first = lax.rem(own - d + devices, devices) * planes + radius
        offset = wrapped(first + (col >> 3) - source_row, depth)
        wf_ref[d] = left_pack(jnp.where(diagonal, by_taps(offset, taps_ref, 0), 0.0))
        offset = wrapped(first + (row >> 3) - source_col, depth)
        wb_ref[d] = left_pack(jnp.where(diagonal, by_taps(offset, taps_ref, 0), 0.0))
        return carry

    lax.fori_loop(0, devices, block, 0)
    yf_ref[...] = row_band(taps_ref, rows, rows + 2 * HALO, HALO - radius, False)
    yi_ref[...] = row_band(taps_ref, inner, rows, HALO + radius, True)
    ye_ref[...] = row_band(taps_ref, HALO, 3 * HALO, HALO + radius, True)
    row = iota((width, width), 0)
    col = iota((width, width), 1)
    xf_ref[...] = right_pack(by_taps(wrapped(row - col + radius, width), taps_ref, 2))
    xb_ref[...] = left_pack(by_taps(wrapped(row - col + radius, width), taps_ref, 2))
    share = width // views
    mine = pl.ds(pl.multiple_of(view * share, share), share)
    for part_ref, old_ref in ((edge_ref, old_edge_ref), (inner_ref, old_inner_ref)):
        pack = LANES // part_ref.shape[1]
        for g in range(planes // pack):
            turned_ref[...] = part_ref[g * pack : (g + 1) * pack].reshape(LANES, width).T
            old_ref[g] = turned_ref[mine, :] * (1.0 / views)


def mix_part(slab_refs, wf_ref, out_refs):
    planes, part_rows, width = slab_refs[0].shape
    cells = planes * 8
    for start in range(0, part_rows, 16):
        total = None
        for d, ref in enumerate(slab_refs):
            cell = jnp.concatenate(
                [ref[:, start + s : start + s + 8, :].reshape(cells, width) for s in (0, 8)], 1
            )
            part = dot(wf_ref[d], split(cell, 0))
            total = part if total is None else total + part
        total = halves(total, 0)
        for s in (0, 8):
            piece = total[:, (s // 8) * width : (s // 8 + 1) * width].reshape(planes, 8, width)
            for ref, at, size in out_refs:
                if at <= start + s < at + size:
                    ref[:, start + s - at : start + s - at + 8, :] = piece


def mix_kernel(blocks, *refs):
    slab_refs, wf_ref, top_ref, bottom_ref = refs[:blocks], *refs[blocks:]
    mix_part(slab_refs, wf_ref, ((top_ref, 0, HALO), (bottom_ref, HALO, HALO)))


def plane_pair(p, pieces):
    return jnp.concatenate([jnp.concatenate([piece(q) for piece in pieces], 0) for q in (p, p + 1)], 1)


def whole(ref):
    return lambda q: ref[q]


def ratio_kernel(blocks, meta_ref, *refs):
    slab_refs = refs[:blocks]
    (
        wf_ref, top_ref, bottom_ref, above_ref, below_ref, measured_ref, yf_ref, xf_ref,
        out_top_ref, out_inner_ref, out_bottom_ref, inner_ref,
    ) = refs[blocks:]
    planes, inner, width = inner_ref.shape
    rows = inner + 2 * HALO
    mix_part(slab_refs, wf_ref, ((inner_ref, 0, inner),))
    depth = (meta_ref.shape[0] - 2) // 2
    base = 2 + depth + meta_ref[0] * planes
    band = yf_ref[...]
    circle = xf_ref[...]
    pieces = [whole(ref) for ref in (above_ref, top_ref, inner_ref, bottom_ref, below_ref)]
    for p in range(0, planes, 2):
        pair = halves(dot(band, split(plane_pair(p, pieces), 0)), 0)
        pair = jnp.concatenate([pair[:, :width], pair[:, width:]], 0)
        pair = halves(dot(split(pair, 1), circle), 1)
        for q in (0, 1):
            shift = meta_ref[base + p + q]
            forward = pltpu.roll(pair[q * rows : (q + 1) * rows], shift, 1)
            ratio = measured_ref[0, p + q] / forward
            ratio = pltpu.roll(ratio, lax.rem(width - shift, width), 1)
            out_top_ref[p + q] = ratio[:HALO]
            out_inner_ref[p + q] = ratio[HALO : rows - HALO]
            out_bottom_ref[p + q] = ratio[rows - HALO :]


def pull_part(rows_ref, wb_ref, out_refs):
    planes, part_rows, width = rows_ref.shape
    cells = planes * 8
    for start in range(0, part_rows, 16):
        cell = jnp.concatenate(
            [rows_ref[:, start + s : start + s + 8, :].reshape(cells, width) for s in (0, 8)], 1
        )
        cell = split(cell, 0)
        for d, out_ref in enumerate(out_refs):
            part = halves(dot(wb_ref[d], cell), 0)
            for s in (0, 8):
                out_ref[:, start + s : start + s + 8, :] = part[
                    :, (s // 8) * width : (s // 8 + 1) * width
                ].reshape(planes, 8, width)


def pull_inner_kernel(top_ref, inner_ref, bottom_ref, yi_ref, wb_ref, *refs):
    out_refs, rows_ref = refs[:-1], refs[-1]
    planes, _, width = inner_ref.shape
    band = yi_ref[...]
    pieces = [whole(ref) for ref in (top_ref, inner_ref, bottom_ref)]
    for p in range(0, planes, 2):
        pair = halves(dot(band, split(plane_pair(p, pieces), 0)), 0)
        rows_ref[p] = pair[:, :width]
        rows_ref[p + 1] = pair[:, width:]
    pull_part(rows_ref, wb_ref, out_refs)


def pull_edge_kernel(top_ref, inner_ref, bottom_ref, above_ref, below_ref, ye_ref, wb_ref, *refs):
    out_refs, rows_ref = refs[:-1], refs[-1]
    planes, inner, width = inner_ref.shape
    band = ye_ref[...]
    for at, pieces in (
        (0, (whole(above_ref), whole(top_ref), lambda q: inner_ref[q, :HALO])),
        (HALO, (lambda q: inner_ref[q, inner - HALO :], whole(bottom_ref), whole(below_ref))),
    ):
        for p in range(0, planes, 2):
            pair = halves(dot(band, split(plane_pair(p, pieces), 0)), 0)
            rows_ref[p, at : at + HALO] = pair[:, :width]
            rows_ref[p + 1, at : at + HALO] = pair[:, width:]
    pull_part(rows_ref, wb_ref, out_refs)


def share_kernel(blocks, views, meta_ref, *refs):
    slab_refs, xb_ref, out_refs, turned_ref = refs[:blocks], refs[blocks], refs[blocks + 1 : -1], refs[-1]
    planes, part_rows, width = slab_refs[0].shape
    view = meta_ref[1]
    share = width // views
    circle = xb_ref[...]
    pack = LANES // part_rows
    for g in range(0, planes // pack, 2):
        total = slab_refs[0][g * pack : (g + 2) * pack]
        for ref in slab_refs[1:]:
            total = total + ref[g * pack : (g + 2) * pack]
        turned = halves(dot(circle, split(total.reshape(2 * LANES, width), 1), 1), 0)
        turned_ref[g] = turned[:, :LANES]
        turned_ref[g + 1] = turned[:, LANES:]
    for k in range(views):
        start = pl.multiple_of(lax.rem(view + k, views) * share, share)
        out_refs[k][...] = turned_ref[:, pl.ds(start, share), :]


def update_kernel(views, old_edge_ref, old_inner_ref, *refs):
    edge_refs, inner_refs, out_ref = refs[:views], refs[views : 2 * views], refs[2 * views]
    groups, share, _ = old_edge_ref.shape
    planes, _, rows = out_ref.shape
    pack = planes // groups
    width = LANES // pack
    for g in range(groups):
        parts = []
        for old_ref, share_refs in ((old_edge_ref, edge_refs), (old_inner_ref, inner_refs)):
            total = share_refs[0][g]
            for ref in share_refs[1:]:
                total = total + ref[g]
            parts.append(total * old_ref[g])
        edge, inner = parts
        for j in range(pack):
            at = j * width
            out_ref[g * pack + j] = jnp.concatenate(
                [edge[:, at : at + HALO], inner[:, at : at + width], edge[:, at + HALO : at + width]], 1
            )


def call(kernel, outs, specs, flops, name, scratch=()):
    spaces = {"s": pltpu.SMEM, "v": pltpu.VMEM}
    vmem = pl.BlockSpec(memory_space=pltpu.VMEM)
    single = not isinstance(outs, (list, tuple))
    return pl.pallas_call(
        kernel,
        out_shape=outs,
        in_specs=[pl.BlockSpec(memory_space=spaces[s]) for s in specs],
        out_specs=vmem if single else [vmem] * len(outs),
        scratch_shapes=list(scratch),
        compiler_params=pltpu.CompilerParams(vmem_limit_bytes=VMEM_LIMIT),
        cost_estimate=pl.CostEstimate(flops=flops, bytes_accessed=1 << 20, transcendentals=0),
        name=name,
    )


def local(estimate, measured, psf_taps, plane_source, plane_shift):
    planes, rows, width = estimate.shape
    devices = lax.axis_size("slab")
    tiles = lax.axis_size("tile")
    views = lax.axis_size("view")
    slab = lax.axis_index("slab")
    view = lax.axis_index("view")
    cells = planes * 8
    inner_rows = rows - 2 * HALO
    share = width // views

    def cells_of(*shape):
        return jax.ShapeDtypeStruct(shape, F32)

    def matrix(*shape):
        return jax.ShapeDtypeStruct(shape, BF16)

    edge = cells_of(planes, HALO, width)
    edges = cells_of(planes, 2 * HALO, width)
    inner = cells_of(planes, inner_rows, width)
    edge_shares = cells_of(planes * 2 * HALO // LANES, share, LANES)
    inner_shares = cells_of(planes * inner_rows // LANES, share, LANES)

    def exchange_rows(top, bottom):
        above = lax.ppermute(bottom, "tile", [(i, (i + 1) % tiles) for i in range(tiles)])
        below = lax.ppermute(top, "tile", [((i + 1) % tiles, i) for i in range(tiles)])
        return above, below

    def to_slabs(parts, step):
        return [parts[0]] + [
            lax.ppermute(parts[d], "slab", [(i, (i + step * d) % devices) for i in range(devices)])
            for d in range(1, devices)
        ]

    def to_views(parts):
        return [parts[0]] + [
            lax.ppermute(parts[k], "view", [(i, (i + k) % views) for i in range(views)])
            for k in range(1, views)
        ]

    own_edge = jnp.concatenate([estimate[:, :HALO], estimate[:, rows - HALO :]], 1)
    own_inner = estimate[:, HALO : rows - HALO]
    edge_slabs = to_slabs([own_edge] * devices, 1)
    inner_slabs = to_slabs([own_inner] * devices, 1)
    kernels = psf_taps[0] / jnp.sum(psf_taps[0], axis=1, keepdims=True)
    meta = jnp.concatenate([jnp.stack([slab, view]).astype(jnp.int32), plane_source[0], plane_shift[0]])
    wf, wb, yf, yi, ye, xf, xb, old_edge, old_inner = call(
        functools.partial(prepare_kernel, devices, views),
        [
            matrix(devices, 2 * cells, 2 * cells),
            matrix(devices, 2 * cells, 2 * cells),
            matrix(2 * rows, 2 * (rows + 2 * HALO)),
            matrix(2 * inner_rows, 2 * rows),
            matrix(2 * HALO, 6 * HALO),
            matrix(2 * width, 2 * width),
            matrix(2 * width, 2 * width),
            edge_shares,
            inner_shares,
        ],
        "ssvv",
        1 << 26,
        "prepare",
        [pltpu.VMEM((width, LANES), F32)],
    )(kernels, meta, own_edge, own_inner)

    top, bottom = call(
        functools.partial(mix_kernel, devices), [edge, edge], "v" * (devices + 1), 1 << 26, "mix_edge"
    )(*edge_slabs, wf)
    above, below = exchange_rows(top, bottom)
    top, middle, bottom = call(
        functools.partial(ratio_kernel, devices),
        [edge, inner, edge],
        "s" + "v" * (devices + 8),
        1 << 28,
        "ratio",
        [pltpu.VMEM((planes, inner_rows, width), F32)],
    )(meta, *inner_slabs, wf, top, bottom, above, below, measured, yf, xf)
    above, below = exchange_rows(top, bottom)
    inner_parts = call(
        pull_inner_kernel,
        [inner] * devices,
        "vvvvv",
        1 << 26,
        "pull_inner",
        [pltpu.VMEM((planes, inner_rows, width), F32)],
    )(top, middle, bottom, yi, wb)
    inner_parts = to_slabs(inner_parts, -1)
    edge_parts = call(
        pull_edge_kernel,
        [edges] * devices,
        "vvvvvvv",
        1 << 26,
        "pull_edge",
        [pltpu.VMEM((planes, 2 * HALO, width), F32)],
    )(top, middle, bottom, above, below, ye, wb)
    edge_parts = to_slabs(edge_parts, -1)

    def shared(parts, shape, name):
        return to_views(
            call(
                functools.partial(share_kernel, devices, views),
                [shape] * views,
                "s" + "v" * (devices + 1),
                1 << 26,
                name,
                [pltpu.VMEM((shape.shape[0], width, LANES), F32)],
            )(meta, *parts, xb)
        )

    inner_sums = shared(inner_parts, inner_shares, "share_inner")
    edge_sums = shared(edge_parts, edge_shares, "share_edge")
    turned = call(
        functools.partial(update_kernel, views),
        cells_of(planes, share, rows),
        "v" * (2 + 2 * views),
        1 << 20,
        "update",
    )(old_edge, old_inner, *edge_sums, *inner_sums)
    return jnp.swapaxes(turned, 1, 2)


def solution(mesh):
    in_specs = (
        P("slab", "tile", None),
        P("view", "slab", "tile", None),
        P("view", None, None),
        P("view", None),
        P("view", None),
    )
    out_specs = P("slab", "tile", "view")
    return jax.shard_map(local, mesh=mesh, in_specs=in_specs, out_specs=out_specs, check_vma=False)
```

```python
import functools

import jax
import jax.numpy as jnp
from jax import lax
from jax.experimental import pallas as pl
from jax.experimental.pallas import tpu as pltpu
from jax.sharding import PartitionSpec as P

F32 = jnp.float32
BF16 = jnp.bfloat16
HALO = 16
LANES = 128
VMEM_LIMIT = 40 * 1024 * 1024


def split(x, axis):
    high = x.astype(BF16)
    low = (x - high.astype(F32)).astype(BF16)
    return jnp.concatenate([high, low], axis)


def dot(a, b, b_axis=0):
    return lax.dot_general(a, b, (((1,), (b_axis,)), ((), ())), preferred_element_type=F32)


def halves(x, axis):
    middle = x.shape[axis] // 2
    return lax.slice_in_dim(x, 0, middle, axis=axis) + lax.slice_in_dim(x, middle, 2 * middle, axis=axis)


def iota(shape, axis):
    return lax.broadcasted_iota(jnp.int32, shape, axis)


def wrapped(offset, length):
    offset = jnp.where(offset < 0, offset + length, offset)
    return jnp.where(offset >= length, offset - length, offset)


def by_taps(offset, taps_ref, axis):
    out = jnp.zeros(offset.shape, F32)
    for t in range(taps_ref.shape[1]):
        out = jnp.where(offset == t, taps_ref[axis, t], out)
    return out


def left_pack(full):
    high = full.astype(BF16)
    low = (full - high.astype(F32)).astype(BF16)
    return jnp.concatenate(
        [jnp.concatenate([high, high], 1), jnp.concatenate([low, jnp.zeros_like(low)], 1)], 0
    )


def right_pack(full):
    high = full.astype(BF16)
    low = (full - high.astype(F32)).astype(BF16)
    return jnp.concatenate(
        [jnp.concatenate([high, low], 1), jnp.concatenate([high, jnp.zeros_like(low)], 1)], 0
    )


def row_band(taps_ref, out_rows, in_rows, lead, back):
    row = iota((out_rows, 2 * in_rows), 0)
    col = iota((out_rows, 2 * in_rows), 1)
    first = col < in_rows
    col = jnp.where(first, col, col - in_rows)
    full = by_taps(row - col + lead if back else col - row - lead, taps_ref, 1)
    high = full.astype(BF16)
    low = jnp.where(first, full - high.astype(F32), 0.0).astype(BF16)
    return jnp.concatenate([high, low], 0)


def plane_maps(devices, planes, meta_ref):
    own = meta_ref[0]
    cells = planes * 8
    row = iota((cells, cells), 0)
    col = iota((cells, cells), 1)
    source_row = jnp.zeros((cells, cells), jnp.int32)
    source_col = jnp.zeros((cells, cells), jnp.int32)
    for p in range(planes):
        source = meta_ref[2 + own * planes + p]
        source_row = jnp.where((row >> 3) == p, source, source_row)
        source_col = jnp.where((col >> 3) == p, source, source_col)
    return row >> 3, col >> 3, (row & 7) == (col & 7), source_row, source_col


def prepare_forward_kernel(devices, taps_ref, meta_ref, inner_ref, wf_ref, yf_ref, xf_ref, inner_out_ref):
    planes, inner, width = inner_ref.shape
    inner_out_ref[...] = inner_ref[...]
    rows = inner + 2 * HALO
    own = meta_ref[0]
    radius = (taps_ref.shape[1] - 1) // 2
    _, col_plane, diagonal, source_row, _ = plane_maps(devices, planes, meta_ref)

    def block(d, carry):
        first = lax.rem(own - d + devices, devices) * planes + radius
        offset = wrapped(first + col_plane - source_row, devices * planes)
        wf_ref[d] = left_pack(jnp.where(diagonal, by_taps(offset, taps_ref, 0), 0.0))
        return carry

    lax.fori_loop(0, devices, block, 0)
    yf_ref[...] = row_band(taps_ref, rows, rows + 2 * HALO, HALO - radius, False)
    offset = iota((width, width), 0) - iota((width, width), 1) + radius
    xf_ref[...] = right_pack(by_taps(wrapped(offset, width), taps_ref, 2))


def prepare_back_kernel(
    devices, views, taps_ref, meta_ref, edge_ref, inner_ref,
    wb_ref, yi_ref, ye_ref, xb_ref, old_edge_ref, old_inner_ref, turned_ref,
):
    planes, inner, width = inner_ref.shape
    rows = inner + 2 * HALO
    own, view = meta_ref[0], meta_ref[1]
    radius = (taps_ref.shape[1] - 1) // 2
    row_plane, _, diagonal, _, source_col = plane_maps(devices, planes, meta_ref)

    def block(d, carry):
        first = lax.rem(own - d + devices, devices) * planes + radius
        offset = wrapped(first + row_plane - source_col, devices * planes)
        wb_ref[d] = left_pack(jnp.where(diagonal, by_taps(offset, taps_ref, 0), 0.0))
        return carry

    lax.fori_loop(0, devices, block, 0)
    yi_ref[...] = row_band(taps_ref, inner, rows, HALO + radius, True)
    ye_ref[...] = row_band(taps_ref, HALO, 3 * HALO, HALO + radius, True)
    share = width // views
    lane = iota((width, width), 1)
    half = lane // (width // 2)
    parity = (view & 1) ^ half
    column = (parity + 2 * ((lane - half * (width // 2)) // share)) * share + lane % share
    offset = column - iota((width, width), 0) + radius
    xb_ref[...] = right_pack(by_taps(wrapped(offset, width), taps_ref, 2))
    mine = pl.ds(pl.multiple_of(view * share, share), share)
    for part_ref, old_ref in ((edge_ref, old_edge_ref), (inner_ref, old_inner_ref)):
        pack = LANES // part_ref.shape[1]
        for g in range(planes // (2 * pack)):
            for odd in (0, 1):
                first = 2 * g * pack + odd
                stack = jnp.concatenate([part_ref[first + 2 * i] for i in range(pack)], 0)
                turned_ref[...] = stack.T
                old_ref[g, odd] = turned_ref[mine, :] * (1.0 / views)


def mix_part(slab_refs, wf_ref, out_refs):
    planes, part_rows, width = slab_refs[0].shape
    cells = planes * 8
    for start in range(0, part_rows, 16):
        total = None
        for d, ref in enumerate(slab_refs):
            cell = jnp.concatenate(
                [ref[:, start + s : start + s + 8, :].reshape(cells, width) for s in (0, 8)], 1
            )
            part = dot(wf_ref[d], split(cell, 0))
            total = part if total is None else total + part
        total = halves(total, 0)
        for s in (0, 8):
            piece = total[:, (s // 8) * width : (s // 8 + 1) * width].reshape(planes, 8, width)
            for ref, at, size in out_refs:
                if at <= start + s < at + size:
                    ref[:, start + s - at : start + s - at + 8, :] = piece


def mix_kernel(blocks, *refs):
    slab_refs, wf_ref, top_ref, bottom_ref = refs[:blocks], *refs[blocks:]
    mix_part(slab_refs, wf_ref, ((top_ref, 0, HALO), (bottom_ref, HALO, HALO)))


def plane_pair(p, pieces):
    return jnp.concatenate([jnp.concatenate([piece(q) for piece in pieces], 0) for q in (p, p + 1)], 1)


def whole(ref):
    return lambda q: ref[q]


def ratio_kernel(blocks, meta_ref, *refs):
    slab_refs = refs[:blocks]
    (
        wf_ref, top_ref, bottom_ref, above_ref, below_ref, measured_ref, yf_ref, xf_ref, _,
        out_top_ref, out_inner_ref, out_bottom_ref, inner_ref, rows_ref,
    ) = refs[blocks:]
    planes, inner, width = inner_ref.shape
    rows = inner + 2 * HALO
    mix_part(slab_refs, wf_ref, ((inner_ref, 0, inner),))
    depth = (meta_ref.shape[0] - 2) // 2
    base = 2 + depth + meta_ref[0] * planes
    band = yf_ref[...]
    pieces = [whole(ref) for ref in (above_ref, top_ref, inner_ref, bottom_ref, below_ref)]
    for p in range(0, planes, 2):
        pair = halves(dot(band, split(plane_pair(p, pieces), 0)), 0)
        rows_ref[p] = pair[:, :width]
        rows_ref[p + 1] = pair[:, width:]
    circle = xf_ref[...]
    for p in range(0, planes, 4):
        four = rows_ref[p : p + 4].reshape(4 * rows, width)
        four = halves(dot(split(four, 1), circle), 1)
        for q in range(4):
            shift = meta_ref[base + p + q]
            forward = pltpu.roll(four[q * rows : (q + 1) * rows], shift, 1)
            ratio = measured_ref[0, p + q] / forward
            ratio = pltpu.roll(ratio, lax.rem(width - shift, width), 1)
            out_top_ref[p + q] = ratio[:HALO]
            out_inner_ref[p + q] = ratio[HALO : rows - HALO]
            out_bottom_ref[p + q] = ratio[rows - HALO :]


def pull_part(rows_ref, xb_ref, wb_ref, out_refs):
    planes, part_rows, width = rows_ref.shape
    cells = planes * 8
    circle = xb_ref[...]
    step = min(planes, 2 * LANES // part_rows)
    for p in range(0, planes, step):
        part = rows_ref[p : p + step].reshape(step * part_rows, width)
        rows_ref[p : p + step] = halves(dot(split(part, 1), circle), 1).reshape(step, part_rows, width)
    left = iota((planes // 2, 8, width), 2) < width // 2
    for start in range(0, part_rows, 16):
        cell = jnp.concatenate(
            [rows_ref[:, start + s : start + s + 8, :].reshape(cells, width) for s in (0, 8)], 1
        )
        cell = split(cell, 0)
        for d in range(len(out_refs) // 2):
            part = halves(dot(wb_ref[d], cell), 0)
            for s in (0, 8):
                piece = part[:, (s // 8) * width : (s // 8 + 1) * width].reshape(planes // 2, 2, 8, width)
                even, odd = piece[:, 0], piece[:, 1]
                at = slice(start + s, start + s + 8)
                out_refs[2 * d][:, at, :] = jnp.where(left, even, pltpu.roll(odd, width // 2, 2))
                out_refs[2 * d + 1][:, at, :] = jnp.where(left, pltpu.roll(even, width // 2, 2), odd)


def pull_inner_kernel(top_ref, inner_ref, bottom_ref, yi_ref, xb_ref, wb_ref, *refs):
    out_refs, rows_ref = refs[:-1], refs[-1]
    planes, _, width = inner_ref.shape
    band = yi_ref[...]
    pieces = [whole(ref) for ref in (top_ref, inner_ref, bottom_ref)]
    for p in range(0, planes, 2):
        pair = halves(dot(band, split(plane_pair(p, pieces), 0)), 0)
        rows_ref[p] = pair[:, :width]
        rows_ref[p + 1] = pair[:, width:]
    pull_part(rows_ref, xb_ref, wb_ref, out_refs)


def pull_edge_kernel(top_ref, inner_ref, bottom_ref, above_ref, below_ref, ye_ref, xb_ref, wb_ref, *refs):
    out_refs, rows_ref = refs[:-1], refs[-1]
    planes, inner, width = inner_ref.shape
    band = ye_ref[...]
    for at, pieces in (
        (0, (whole(above_ref), whole(top_ref), lambda q: inner_ref[q, :HALO])),
        (HALO, (lambda q: inner_ref[q, inner - HALO :], whole(bottom_ref), whole(below_ref))),
    ):
        for p in range(0, planes, 2):
            pair = halves(dot(band, split(plane_pair(p, pieces), 0)), 0)
            rows_ref[p, at : at + HALO] = pair[:, :width]
            rows_ref[p + 1, at : at + HALO] = pair[:, width:]
    pull_part(rows_ref, xb_ref, wb_ref, out_refs)


def gather_kernel(blocks, views, meta_ref, *refs):
    part_refs, out_refs, turned_ref = refs[:blocks], refs[blocks:-1], refs[-1]
    pairs, part_rows, width = part_refs[0].shape
    share = width // views
    pack = LANES // part_rows
    for g in range(pairs // pack):
        total = part_refs[0][g * pack : (g + 1) * pack]
        for ref in part_refs[1:]:
            total = total + ref[g * pack : (g + 1) * pack]
        turned_ref[g] = total.reshape(LANES, width).T
    for k in range(views // 2):
        start = lax.rem(meta_ref[1] // 2 + k, views // 2) * share
        for odd in (0, 1):
            at = pl.multiple_of(odd * (width // 2) + start, share)
            out_refs[k][:, odd] = turned_ref[:, pl.ds(at, share), :]


def update_kernel(count, old_edge_ref, old_inner_ref, *refs):
    edge_refs, inner_refs, out_ref = refs[:count], refs[count : 2 * count], refs[2 * count]
    groups, _, share, _ = old_edge_ref.shape
    planes, _, rows = out_ref.shape
    pack = planes // (2 * groups)
    width = LANES // pack
    for g in range(groups):
        for odd in (0, 1):
            parts = []
            for old_ref, share_refs in ((old_edge_ref, edge_refs), (old_inner_ref, inner_refs)):
                total = share_refs[0][g, odd]
                for ref in share_refs[1:]:
                    total = total + ref[g, odd]
                parts.append(total * old_ref[g, odd])
            edge, inner = parts
            for i in range(pack):
                at = i * width
                out_ref[2 * (g * pack + i) + odd] = jnp.concatenate(
                    [edge[:, at : at + HALO], inner[:, at : at + width], edge[:, at + HALO : at + width]], 1
                )


def call(kernel, outs, specs, flops, name, scratch=()):
    spaces = {"s": pltpu.SMEM, "v": pltpu.VMEM}
    vmem = pl.BlockSpec(memory_space=pltpu.VMEM)
    single = not isinstance(outs, (list, tuple))
    return pl.pallas_call(
        kernel,
        out_shape=outs,
        in_specs=[pl.BlockSpec(memory_space=spaces[s]) for s in specs],
        out_specs=vmem if single else [vmem] * len(outs),
        scratch_shapes=list(scratch),
        compiler_params=pltpu.CompilerParams(vmem_limit_bytes=VMEM_LIMIT),
        cost_estimate=pl.CostEstimate(flops=flops, bytes_accessed=1 << 20, transcendentals=0),
        name=name,
    )


def local(estimate, measured, psf_taps, plane_source, plane_shift):
    planes, rows, width = estimate.shape
    devices = lax.axis_size("slab")
    tiles = lax.axis_size("tile")
    views = lax.axis_size("view")
    slab = lax.axis_index("slab")
    view = lax.axis_index("view")
    cells = planes * 8
    inner_rows = rows - 2 * HALO
    share = width // views

    def cells_of(*shape):
        return jax.ShapeDtypeStruct(shape, F32)

    def matrix(*shape):
        return jax.ShapeDtypeStruct(shape, BF16)

    edge = cells_of(planes, HALO, width)
    edges = cells_of(planes, 2 * HALO, width)
    inner = cells_of(planes, inner_rows, width)
    edge_pairs = cells_of(planes // 2, 2 * HALO, width)
    inner_pairs = cells_of(planes // 2, inner_rows, width)
    edge_shares = cells_of(planes * HALO // LANES, 2, share, LANES)
    inner_shares = cells_of(planes * inner_rows // (2 * LANES), 2, share, LANES)

    def exchange_rows(top, bottom):
        above = lax.ppermute(bottom, "tile", [(i, (i + 1) % tiles) for i in range(tiles)])
        below = lax.ppermute(top, "tile", [((i + 1) % tiles, i) for i in range(tiles)])
        return above, below

    def all_slabs(part):
        return [part] + [
            lax.ppermute(part, "slab", [(i, (i + d) % devices) for i in range(devices)])
            for d in range(1, devices)
        ]

    def to_pairs(parts):
        return [parts[0]] + [
            lax.ppermute(
                parts[2 * d + e],
                ("slab", "view"),
                [
                    (i * views + v, (i - d) % devices * views + (v ^ e))
                    for i in range(devices)
                    for v in range(views)
                ],
            )
            for d in reversed(range(devices))
            for e in (1, 0)
            if d + e
        ]

    def to_views(parts):
        return [parts[0]] + [
            lax.ppermute(parts[k], "view", [(i, (i + 2 * k) % views) for i in range(views)])
            for k in range(1, views // 2)
        ]

    own_edge = jnp.concatenate([estimate[:, :HALO], estimate[:, rows - HALO :]], 1)
    own_inner = estimate[:, HALO : rows - HALO]
    edge_slabs = all_slabs(own_edge)
    kernels = psf_taps[0] / jnp.sum(psf_taps[0], axis=1, keepdims=True)
    meta = jnp.concatenate([jnp.stack([slab, view]).astype(jnp.int32), plane_source[0], plane_shift[0]])
    wf, yf, xf, own_inner = call(
        functools.partial(prepare_forward_kernel, devices),
        [
            matrix(devices, 2 * cells, 2 * cells),
            matrix(2 * rows, 2 * (rows + 2 * HALO)),
            matrix(2 * width, 2 * width),
            inner,
        ],
        "ssv",
        1 << 26,
        "prepare_forward",
    )(kernels, meta, own_inner)
    inner_slabs = all_slabs(own_inner)
    wb, yi, ye, xb, old_edge, old_inner = call(
        functools.partial(prepare_back_kernel, devices, views),
        [
            matrix(devices, 2 * cells, 2 * cells),
            matrix(2 * inner_rows, 2 * rows),
            matrix(2 * HALO, 6 * HALO),
            matrix(2 * width, 2 * width),
            edge_shares,
            inner_shares,
        ],
        "ssvv",
        1 << 26,
        "prepare_back",
        [pltpu.VMEM((width, LANES), F32)],
    )(kernels, meta, own_edge, own_inner)

    top, bottom = call(
        functools.partial(mix_kernel, devices), [edge, edge], "v" * (devices + 1), 1 << 26, "mix_edge"
    )(*edge_slabs, wf)
    above, below = exchange_rows(top, bottom)
    top, middle, bottom = call(
        functools.partial(ratio_kernel, devices),
        [edge, inner, edge],
        "s" + "v" * (devices + 9),
        1 << 28,
        "ratio",
        [pltpu.VMEM((planes, inner_rows, width), F32), pltpu.VMEM((planes, rows, width), F32)],
    )(meta, *inner_slabs, wf, top, bottom, above, below, measured, yf, xf, ye)
    above, below = exchange_rows(top, bottom)
    inner_parts = call(
        pull_inner_kernel,
        [inner_pairs] * (2 * devices),
        "v" * 6,
        1 << 26,
        "pull_inner",
        [pltpu.VMEM((planes, inner_rows, width), F32)],
    )(top, middle, bottom, yi, xb, wb)
    inner_parts = to_pairs(inner_parts)
    edge_parts = call(
        pull_edge_kernel,
        [edge_pairs] * (2 * devices),
        "v" * 8,
        1 << 26,
        "pull_edge",
        [pltpu.VMEM((planes, 2 * HALO, width), F32)],
    )(top, middle, bottom, above, below, ye, xb, wb)
    edge_parts = to_pairs(edge_parts)

    def gathered(parts, shape, name):
        return to_views(
            call(
                functools.partial(gather_kernel, 2 * devices, views),
                [shape] * (views // 2),
                "s" + "v" * (2 * devices),
                1 << 24,
                name,
                [pltpu.VMEM((shape.shape[0], width, LANES), F32)],
            )(meta, *parts)
        )

    inner_sums = gathered(inner_parts, inner_shares, "gather_inner")
    edge_sums = gathered(edge_parts, edge_shares, "gather_edge")
    turned = call(
        functools.partial(update_kernel, views // 2),
        cells_of(planes, share, rows),
        "v" * (2 + views),
        1 << 20,
        "update",
    )(old_edge, old_inner, *edge_sums, *inner_sums)
    return jnp.swapaxes(turned, 1, 2)


def solution(mesh):
    in_specs = (
        P("slab", "tile", None),
        P("view", "slab", "tile", None),
        P("view", None, None),
        P("view", None),
        P("view", None),
    )
    out_specs = P("slab", "tile", "view")
    return jax.shard_map(local, mesh=mesh, in_specs=in_specs, out_specs=out_specs, check_vma=False)
```

```python
import functools

import jax
import jax.numpy as jnp
from jax import lax
from jax.experimental import pallas as pl
from jax.experimental.pallas import tpu as pltpu
from jax.sharding import PartitionSpec as P

F32 = jnp.float32
BF16 = jnp.bfloat16
HALO = 16
LANES = 128
VMEM_LIMIT = 40 * 1024 * 1024


def split(x, axis):
    high = x.astype(BF16)
    low = (x - high.astype(F32)).astype(BF16)
    return jnp.concatenate([high, low], axis)


def dot(a, b, b_axis=0):
    return lax.dot_general(a, b, (((1,), (b_axis,)), ((), ())), preferred_element_type=F32)


def halves(x, axis):
    middle = x.shape[axis] // 2
    return lax.slice_in_dim(x, 0, middle, axis=axis) + lax.slice_in_dim(x, middle, 2 * middle, axis=axis)


def iota(shape, axis):
    return lax.broadcasted_iota(jnp.int32, shape, axis)


def wrapped(offset, length):
    offset = jnp.where(offset < 0, offset + length, offset)
    return jnp.where(offset >= length, offset - length, offset)


def by_taps(offset, taps_ref, axis):
    out = jnp.zeros(offset.shape, F32)
    for t in range(taps_ref.shape[1]):
        out = jnp.where(offset == t, taps_ref[axis, t], out)
    return out


def left_pack(full):
    high = full.astype(BF16)
    low = (full - high.astype(F32)).astype(BF16)
    return jnp.concatenate(
        [jnp.concatenate([high, high], 1), jnp.concatenate([low, jnp.zeros_like(low)], 1)], 0
    )


def right_pack(full):
    high = full.astype(BF16)
    low = (full - high.astype(F32)).astype(BF16)
    return jnp.concatenate(
        [jnp.concatenate([high, low], 1), jnp.concatenate([high, jnp.zeros_like(low)], 1)], 0
    )


def row_band(taps_ref, out_rows, in_rows, lead, back):
    row = iota((out_rows, 2 * in_rows), 0)
    col = iota((out_rows, 2 * in_rows), 1)
    first = col < in_rows
    col = jnp.where(first, col, col - in_rows)
    full = by_taps(row - col + lead if back else col - row - lead, taps_ref, 1)
    high = full.astype(BF16)
    low = jnp.where(first, full - high.astype(F32), 0.0).astype(BF16)
    return jnp.concatenate([high, low], 0)


def plane_maps(devices, planes, meta_ref):
    own = meta_ref[0]
    cells = planes * 8
    row = iota((cells, cells), 0)
    col = iota((cells, cells), 1)
    source_row = jnp.zeros((cells, cells), jnp.int32)
    source_col = jnp.zeros((cells, cells), jnp.int32)
    for p in range(planes):
        source = meta_ref[2 + own * planes + p]
        source_row = jnp.where((row >> 3) == p, source, source_row)
        source_col = jnp.where((col >> 3) == p, source, source_col)
    return row >> 3, col >> 3, (row & 7) == (col & 7), source_row, source_col


def prepare_forward_kernel(devices, taps_ref, meta_ref, inner_ref, wf_ref, yf_ref, xf_ref):
    planes, inner, width = inner_ref.shape
    rows = inner + 2 * HALO
    own = meta_ref[0]
    radius = (taps_ref.shape[1] - 1) // 2
    _, col_plane, diagonal, source_row, _ = plane_maps(devices, planes, meta_ref)

    def block(d, carry):
        first = lax.rem(own - d + devices, devices) * planes + radius
        offset = wrapped(first + col_plane - source_row, devices * planes)
        wf_ref[d] = left_pack(jnp.where(diagonal, by_taps(offset, taps_ref, 0), 0.0))
        return carry

    lax.fori_loop(0, devices, block, 0)
    yf_ref[...] = row_band(taps_ref, rows, rows + 2 * HALO, HALO - radius, False)
    offset = iota((width, width), 0) - iota((width, width), 1) + radius
    xf_ref[...] = right_pack(by_taps(wrapped(offset, width), taps_ref, 2))


def prepare_back_kernel(
    devices, views, taps_ref, meta_ref, edge_ref, inner_ref, _,
    wb_ref, yi_ref, ye_ref, xb_ref, old_edge_ref, old_inner_ref, inner_out_ref, turned_ref,
):
    planes, inner, width = inner_ref.shape
    inner_out_ref[...] = inner_ref[...]
    rows = inner + 2 * HALO
    own, view = meta_ref[0], meta_ref[1]
    radius = (taps_ref.shape[1] - 1) // 2
    row_plane, _, diagonal, _, source_col = plane_maps(devices, planes, meta_ref)

    def block(d, carry):
        first = lax.rem(own - d + devices, devices) * planes + radius
        offset = wrapped(first + row_plane - source_col, devices * planes)
        wb_ref[d] = left_pack(jnp.where(diagonal, by_taps(offset, taps_ref, 0), 0.0))
        return carry

    lax.fori_loop(0, devices, block, 0)
    yi_ref[...] = row_band(taps_ref, inner, rows, HALO + radius, True)
    ye_ref[...] = row_band(taps_ref, HALO, 3 * HALO, HALO + radius, True)
    share = width // views
    lane = iota((width, width), 1)
    half = lane // (width // 2)
    parity = (view & 1) ^ half
    column = (parity + 2 * ((lane - half * (width // 2)) // share)) * share + lane % share
    offset = column - iota((width, width), 0) + radius
    xb_ref[...] = right_pack(by_taps(wrapped(offset, width), taps_ref, 2))
    mine = pl.ds(pl.multiple_of(view * share, share), share)
    for part_ref, old_ref in ((edge_ref, old_edge_ref), (inner_ref, old_inner_ref)):
        pack = LANES // part_ref.shape[1]
        for g in range(planes // (2 * pack)):
            for odd in (0, 1):
                first = 2 * g * pack + odd
                stack = jnp.concatenate([part_ref[first + 2 * i] for i in range(pack)], 0)
                turned_ref[...] = stack.T
                old_ref[g, odd] = turned_ref[mine, :] * (1.0 / views)


def mix_part(slab_refs, wf_ref, out_refs):
    planes, part_rows, width = slab_refs[0].shape
    cells = planes * 8
    for start in range(0, part_rows, 16):
        total = None
        for d, ref in enumerate(slab_refs):
            cell = jnp.concatenate(
                [ref[:, start + s : start + s + 8, :].reshape(cells, width) for s in (0, 8)], 1
            )
            part = dot(wf_ref[d], split(cell, 0))
            total = part if total is None else total + part
        total = halves(total, 0)
        for s in (0, 8):
            piece = total[:, (s // 8) * width : (s // 8 + 1) * width].reshape(planes, 8, width)
            for ref, at, size in out_refs:
                if at <= start + s < at + size:
                    ref[:, start + s - at : start + s - at + 8, :] = piece


def mix_kernel(blocks, *refs):
    slab_refs, wf_ref, top_ref, bottom_ref = refs[:blocks], *refs[blocks:]
    mix_part(slab_refs, wf_ref, ((top_ref, 0, HALO), (bottom_ref, HALO, HALO)))


def plane_pair(p, pieces):
    return jnp.concatenate([jnp.concatenate([piece(q) for piece in pieces], 0) for q in (p, p + 1)], 1)


def whole(ref):
    return lambda q: ref[q]


def ratio_kernel(blocks, meta_ref, *refs):
    slab_refs = refs[:blocks]
    (
        wf_ref, top_ref, bottom_ref, above_ref, below_ref, measured_ref, yf_ref, xf_ref,
        out_top_ref, out_inner_ref, out_bottom_ref, inner_ref, rows_ref,
    ) = refs[blocks:]
    planes, inner, width = inner_ref.shape
    rows = inner + 2 * HALO
    mix_part(slab_refs, wf_ref, ((inner_ref, 0, inner),))
    depth = (meta_ref.shape[0] - 2) // 2
    base = 2 + depth + meta_ref[0] * planes
    band = yf_ref[...]
    pieces = [whole(ref) for ref in (above_ref, top_ref, inner_ref, bottom_ref, below_ref)]
    for p in range(0, planes, 2):
        pair = halves(dot(band, split(plane_pair(p, pieces), 0)), 0)
        rows_ref[p] = pair[:, :width]
        rows_ref[p + 1] = pair[:, width:]
    circle = xf_ref[...]
    for p in range(0, planes, 4):
        four = rows_ref[p : p + 4].reshape(4 * rows, width)
        four = halves(dot(split(four, 1), circle), 1)
        for q in range(4):
            shift = meta_ref[base + p + q]
            forward = pltpu.roll(four[q * rows : (q + 1) * rows], shift, 1)
            inverse = pl.reciprocal(forward, approx=True)
            for _ in range(2):
                inverse = inverse * (2.0 - forward * inverse)
            ratio = measured_ref[0, p + q] * inverse
            ratio = pltpu.roll(ratio, lax.rem(width - shift, width), 1)
            out_top_ref[p + q] = ratio[:HALO]
            out_inner_ref[p + q] = ratio[HALO : rows - HALO]
            out_bottom_ref[p + q] = ratio[rows - HALO :]


def pull_part(rows_ref, xb_ref, wb_ref, out_refs):
    planes, part_rows, width = rows_ref.shape
    cells = planes * 8
    circle = xb_ref[...]
    step = min(planes, 2 * LANES // part_rows)
    for p in range(0, planes, step):
        part = rows_ref[p : p + step].reshape(step * part_rows, width)
        rows_ref[p : p + step] = halves(dot(split(part, 1), circle), 1).reshape(step, part_rows, width)
    left = iota((planes // 2, 8, width), 2) < width // 2
    for start in range(0, part_rows, 16):
        cell = jnp.concatenate(
            [rows_ref[:, start + s : start + s + 8, :].reshape(cells, width) for s in (0, 8)], 1
        )
        cell = split(cell, 0)
        for d in range(len(out_refs) // 2):
            part = halves(dot(wb_ref[d], cell), 0)
            for s in (0, 8):
                piece = part[:, (s // 8) * width : (s // 8 + 1) * width].reshape(planes // 2, 2, 8, width)
                even, odd = piece[:, 0], piece[:, 1]
                at = slice(start + s, start + s + 8)
                out_refs[2 * d][:, at, :] = jnp.where(left, even, pltpu.roll(odd, width // 2, 2))
                out_refs[2 * d + 1][:, at, :] = jnp.where(left, pltpu.roll(even, width // 2, 2), odd)


def pull_inner_kernel(top_ref, inner_ref, bottom_ref, yi_ref, xb_ref, wb_ref, *refs):
    out_refs, rows_ref = refs[:-1], refs[-1]
    planes, _, width = inner_ref.shape
    band = yi_ref[...]
    pieces = [whole(ref) for ref in (top_ref, inner_ref, bottom_ref)]
    for p in range(0, planes, 2):
        pair = halves(dot(band, split(plane_pair(p, pieces), 0)), 0)
        rows_ref[p] = pair[:, :width]
        rows_ref[p + 1] = pair[:, width:]
    pull_part(rows_ref, xb_ref, wb_ref, out_refs)


def pull_edge_kernel(top_ref, inner_ref, bottom_ref, above_ref, below_ref, ye_ref, xb_ref, wb_ref, *refs):
    out_refs, rows_ref = refs[:-1], refs[-1]
    planes, inner, width = inner_ref.shape
    band = ye_ref[...]
    for at, pieces in (
        (0, (whole(above_ref), whole(top_ref), lambda q: inner_ref[q, :HALO])),
        (HALO, (lambda q: inner_ref[q, inner - HALO :], whole(bottom_ref), whole(below_ref))),
    ):
        for p in range(0, planes, 2):
            pair = halves(dot(band, split(plane_pair(p, pieces), 0)), 0)
            rows_ref[p, at : at + HALO] = pair[:, :width]
            rows_ref[p + 1, at : at + HALO] = pair[:, width:]
    pull_part(rows_ref, xb_ref, wb_ref, out_refs)


def gather_kernel(blocks, views, meta_ref, *refs):
    part_refs, out_refs, turned_ref = refs[:blocks], refs[blocks:-1], refs[-1]
    pairs, part_rows, width = part_refs[0].shape
    share = width // views
    pack = LANES // part_rows
    for g in range(pairs // pack):
        total = part_refs[0][g * pack : (g + 1) * pack]
        for ref in part_refs[1:]:
            total = total + ref[g * pack : (g + 1) * pack]
        turned_ref[g] = total.reshape(LANES, width).T
    for k in range(views // 2):
        start = lax.rem(meta_ref[1] // 2 + k, views // 2) * share
        for odd in (0, 1):
            at = pl.multiple_of(odd * (width // 2) + start, share)
            out_refs[k][:, odd] = turned_ref[:, pl.ds(at, share), :]


def update_kernel(count, old_edge_ref, old_inner_ref, *refs):
    edge_refs, inner_refs, out_ref = refs[:count], refs[count : 2 * count], refs[2 * count]
    groups, _, share, _ = old_edge_ref.shape
    planes, _, rows = out_ref.shape
    pack = planes // (2 * groups)
    width = LANES // pack
    for g in range(groups):
        for odd in (0, 1):
            parts = []
            for old_ref, share_refs in ((old_edge_ref, edge_refs), (old_inner_ref, inner_refs)):
                total = share_refs[0][g, odd]
                for ref in share_refs[1:]:
                    total = total + ref[g, odd]
                parts.append(total * old_ref[g, odd])
            edge, inner = parts
            for i in range(pack):
                at = i * width
                out_ref[2 * (g * pack + i) + odd] = jnp.concatenate(
                    [edge[:, at : at + HALO], inner[:, at : at + width], edge[:, at + HALO : at + width]], 1
                )


def call(kernel, outs, specs, flops, name, scratch=()):
    spaces = {"s": pltpu.SMEM, "v": pltpu.VMEM}
    vmem = pl.BlockSpec(memory_space=pltpu.VMEM)
    single = not isinstance(outs, (list, tuple))
    return pl.pallas_call(
        kernel,
        out_shape=outs,
        in_specs=[pl.BlockSpec(memory_space=spaces[s]) for s in specs],
        out_specs=vmem if single else [vmem] * len(outs),
        scratch_shapes=list(scratch),
        compiler_params=pltpu.CompilerParams(vmem_limit_bytes=VMEM_LIMIT),
        cost_estimate=pl.CostEstimate(flops=flops, bytes_accessed=1 << 20, transcendentals=0),
        name=name,
    )


def local(estimate, measured, psf_taps, plane_source, plane_shift):
    planes, rows, width = estimate.shape
    devices = lax.axis_size("slab")
    tiles = lax.axis_size("tile")
    views = lax.axis_size("view")
    slab = lax.axis_index("slab")
    view = lax.axis_index("view")
    cells = planes * 8
    inner_rows = rows - 2 * HALO
    share = width // views

    def cells_of(*shape):
        return jax.ShapeDtypeStruct(shape, F32)

    def matrix(*shape):
        return jax.ShapeDtypeStruct(shape, BF16)

    edge = cells_of(planes, HALO, width)
    edges = cells_of(planes, 2 * HALO, width)
    inner = cells_of(planes, inner_rows, width)
    edge_pairs = cells_of(planes // 2, 2 * HALO, width)
    inner_pairs = cells_of(planes // 2, inner_rows, width)
    edge_shares = cells_of(planes * HALO // LANES, 2, share, LANES)
    inner_shares = cells_of(planes * inner_rows // (2 * LANES), 2, share, LANES)

    def exchange_rows(top, bottom):
        above = lax.ppermute(bottom, "tile", [(i, (i + 1) % tiles) for i in range(tiles)])
        below = lax.ppermute(top, "tile", [((i + 1) % tiles, i) for i in range(tiles)])
        return above, below

    def all_slabs(part):
        return [part] + [
            lax.ppermute(part, "slab", [(i, (i + d) % devices) for i in range(devices)])
            for d in range(1, devices)
        ]

    def to_pairs(parts):
        return [parts[0]] + [
            lax.ppermute(
                parts[2 * d + e],
                ("slab", "view"),
                [
                    (i * views + v, (i - d) % devices * views + (v ^ e))
                    for i in range(devices)
                    for v in range(views)
                ],
            )
            for d in reversed(range(devices))
            for e in (1, 0)
            if d + e
        ]

    def to_views(parts):
        return [parts[0]] + [
            lax.ppermute(parts[k], "view", [(i, (i + 2 * k) % views) for i in range(views)])
            for k in range(1, views // 2)
        ]

    own_edge = jnp.concatenate([estimate[:, :HALO], estimate[:, rows - HALO :]], 1)
    own_inner = estimate[:, HALO : rows - HALO]
    edge_slabs = all_slabs(own_edge)
    kernels = psf_taps[0] / jnp.sum(psf_taps[0], axis=1, keepdims=True)
    meta = jnp.concatenate([jnp.stack([slab, view]).astype(jnp.int32), plane_source[0], plane_shift[0]])
    wf, yf, xf = call(
        functools.partial(prepare_forward_kernel, devices),
        [
            matrix(devices, 2 * cells, 2 * cells),
            matrix(2 * rows, 2 * (rows + 2 * HALO)),
            matrix(2 * width, 2 * width),
        ],
        "ssv",
        1 << 26,
        "prepare_forward",
    )(kernels, meta, own_inner)
    wb, yi, ye, xb, old_edge, old_inner, own_inner = call(
        functools.partial(prepare_back_kernel, devices, views),
        [
            matrix(devices, 2 * cells, 2 * cells),
            matrix(2 * inner_rows, 2 * rows),
            matrix(2 * HALO, 6 * HALO),
            matrix(2 * width, 2 * width),
            edge_shares,
            inner_shares,
            inner,
        ],
        "ssvvv",
        1 << 26,
        "prepare_back",
        [pltpu.VMEM((width, LANES), F32)],
    )(kernels, meta, own_edge, own_inner, yf)
    inner_slabs = all_slabs(own_inner)

    top, bottom = call(
        functools.partial(mix_kernel, devices), [edge, edge], "v" * (devices + 1), 1 << 26, "mix_edge"
    )(*edge_slabs, wf)
    above, below = exchange_rows(top, bottom)
    top, middle, bottom = call(
        functools.partial(ratio_kernel, devices),
        [edge, inner, edge],
        "s" + "v" * (devices + 8),
        1 << 28,
        "ratio",
        [pltpu.VMEM((planes, inner_rows, width), F32), pltpu.VMEM((planes, rows, width), F32)],
    )(meta, *inner_slabs, wf, top, bottom, above, below, measured, yf, xf)
    above, below = exchange_rows(top, bottom)
    inner_parts = call(
        pull_inner_kernel,
        [inner_pairs] * (2 * devices),
        "v" * 6,
        1 << 26,
        "pull_inner",
        [pltpu.VMEM((planes, inner_rows, width), F32)],
    )(top, middle, bottom, yi, xb, wb)
    inner_parts = to_pairs(inner_parts)
    edge_parts = call(
        pull_edge_kernel,
        [edge_pairs] * (2 * devices),
        "v" * 8,
        1 << 26,
        "pull_edge",
        [pltpu.VMEM((planes, 2 * HALO, width), F32)],
    )(top, middle, bottom, above, below, ye, xb, wb)
    edge_parts = to_pairs(edge_parts)

    def gathered(parts, shape, name):
        return to_views(
            call(
                functools.partial(gather_kernel, 2 * devices, views),
                [shape] * (views // 2),
                "s" + "v" * (2 * devices),
                1 << 24,
                name,
                [pltpu.VMEM((shape.shape[0], width, LANES), F32)],
            )(meta, *parts)
        )

    inner_sums = gathered(inner_parts, inner_shares, "gather_inner")
    edge_sums = gathered(edge_parts, edge_shares, "gather_edge")
    turned = call(
        functools.partial(update_kernel, views // 2),
        cells_of(planes, share, rows),
        "v" * (2 + views),
        1 << 20,
        "update",
    )(old_edge, old_inner, *edge_sums, *inner_sums)
    return jnp.swapaxes(turned, 1, 2)


def solution(mesh):
    in_specs = (
        P("slab", "tile", None),
        P("view", "slab", "tile", None),
        P("view", None, None),
        P("view", None),
        P("view", None),
    )
    out_specs = P("slab", "tile", "view")
    return jax.shard_map(local, mesh=mesh, in_specs=in_specs, out_specs=out_specs, check_vma=False)
```

```python
import functools

import jax
import jax.numpy as jnp
from jax import lax
from jax.experimental import pallas as pl
from jax.experimental.pallas import tpu as pltpu
from jax.sharding import PartitionSpec as P

F32 = jnp.float32
BF16 = jnp.bfloat16
HALO = 16
VMEM_LIMIT = 40 * 1024 * 1024


def split(x, axis):
    high = x.astype(BF16)
    low = (x - high.astype(F32)).astype(BF16)
    return jnp.concatenate([high, low], axis)


def dot(a, b, b_axis=0):
    return lax.dot_general(a, b, (((1,), (b_axis,)), ((), ())), preferred_element_type=F32)


def halves(x, axis):
    middle = x.shape[axis] // 2
    return lax.slice_in_dim(x, 0, middle, axis=axis) + lax.slice_in_dim(x, middle, 2 * middle, axis=axis)


def iota(shape, axis):
    return lax.broadcasted_iota(jnp.int32, shape, axis)


def wrapped(offset, length):
    offset = jnp.where(offset < 0, offset + length, offset)
    return jnp.where(offset >= length, offset - length, offset)


def by_taps(offset, taps_ref, axis):
    out = jnp.zeros(offset.shape, F32)
    for t in range(taps_ref.shape[1]):
        out = jnp.where(offset == t, taps_ref[axis, t], out)
    return out


def left_pack(full):
    high = full.astype(BF16)
    low = (full - high.astype(F32)).astype(BF16)
    return jnp.concatenate(
        [jnp.concatenate([high, high], 1), jnp.concatenate([low, jnp.zeros_like(low)], 1)], 0
    )


def right_pack(full):
    high = full.astype(BF16)
    low = (full - high.astype(F32)).astype(BF16)
    return jnp.concatenate(
        [jnp.concatenate([high, low], 1), jnp.concatenate([high, jnp.zeros_like(low)], 1)], 0
    )


def row_band(taps_ref, out_rows, in_rows, lead, back):
    row = iota((out_rows, 2 * in_rows), 0)
    col = iota((out_rows, 2 * in_rows), 1)
    first = col < in_rows
    col = jnp.where(first, col, col - in_rows)
    full = by_taps(row - col + lead if back else col - row - lead, taps_ref, 1)
    high = full.astype(BF16)
    low = jnp.where(first, full - high.astype(F32), 0.0).astype(BF16)
    return jnp.concatenate([high, low], 0)


def plane_maps(devices, planes, meta_ref):
    own = meta_ref[0]
    cells = planes * 8
    row = iota((cells, cells), 0)
    col = iota((cells, cells), 1)
    source_row = jnp.zeros((cells, cells), jnp.int32)
    for p in range(planes):
        source_row = jnp.where((row >> 3) == p, meta_ref[2 + own * planes + p], source_row)
    return col >> 3, (row & 7) == (col & 7), source_row


def prepare_forward_kernel(devices, taps_ref, meta_ref, inner_ref, wf_ref, yf_ref, xf_ref):
    planes, inner, width = inner_ref.shape
    rows = inner + 2 * HALO
    own = meta_ref[0]
    radius = (taps_ref.shape[1] - 1) // 2
    col_plane, diagonal, source_row = plane_maps(devices, planes, meta_ref)

    def block(d, carry):
        first = lax.rem(own - d + devices, devices) * planes + radius
        offset = wrapped(first + col_plane - source_row, devices * planes)
        wf_ref[d] = left_pack(jnp.where(diagonal, by_taps(offset, taps_ref, 0), 0.0))
        return carry

    lax.fori_loop(0, devices, block, 0)
    yf_ref[...] = row_band(taps_ref, rows, rows + 2 * HALO, HALO - radius, False)
    offset = iota((width, width), 0) - iota((width, width), 1) + radius
    xf_ref[...] = right_pack(by_taps(wrapped(offset, width), taps_ref, 2))


def prepare_back_kernel(
    devices, views, taps_ref, meta_ref, edge_ref, inner_ref, _,
    wb_ref, yi_ref, ye_ref, xb_ref, old_edge_ref, old_inner_ref, inner_out_ref, turned_ref,
):
    planes, inner, width = inner_ref.shape
    inner_out_ref[...] = inner_ref[...]
    rows = inner + 2 * HALO
    own, view = meta_ref[0], meta_ref[1]
    radius = (taps_ref.shape[1] - 1) // 2
    col_plane, diagonal, source_row = plane_maps(devices, planes, meta_ref)

    def block(d, carry):
        first = lax.rem(own - d + devices, devices) * planes + radius
        offset = wrapped(first + col_plane - source_row, devices * planes)
        wb_ref[d] = right_pack(jnp.where(diagonal, by_taps(offset, taps_ref, 0), 0.0))
        return carry

    lax.fori_loop(0, devices, block, 0)
    yi_ref[...] = row_band(taps_ref, inner, rows, HALO + radius, True)
    ye_ref[...] = row_band(taps_ref, HALO, 3 * HALO, HALO + radius, True)
    share = width // views
    row = iota((width, width), 0)
    half = row // (width // 2)
    parity = (view & 1) ^ half
    column = (parity + 2 * ((row - half * (width // 2)) // share)) * share + row % share
    offset = column - iota((width, width), 1) + radius
    xb_ref[...] = left_pack(by_taps(wrapped(offset, width), taps_ref, 2))
    mine = pl.ds(pl.multiple_of(view * share, share), share)
    for part_ref, old_ref in ((edge_ref, old_edge_ref), (inner_ref, old_inner_ref)):
        for g in range(part_ref.shape[1] // 8):
            turned_ref[...] = part_ref[:, g * 8 : g * 8 + 8, :].reshape(planes * 8, width).T
            old_ref[g] = turned_ref[mine, :] * (1.0 / views)


def mix_part(slab_refs, wf_ref, out_refs):
    planes, part_rows, width = slab_refs[0].shape
    cells = planes * 8
    for start in range(0, part_rows, 16):
        total = None
        for d, ref in enumerate(slab_refs):
            cell = jnp.concatenate(
                [ref[:, start + s : start + s + 8, :].reshape(cells, width) for s in (0, 8)], 1
            )
            part = dot(wf_ref[d], split(cell, 0))
            total = part if total is None else total + part
        total = halves(total, 0)
        for s in (0, 8):
            piece = total[:, (s // 8) * width : (s // 8 + 1) * width].reshape(planes, 8, width)
            for ref, at, size in out_refs:
                if at <= start + s < at + size:
                    ref[:, start + s - at : start + s - at + 8, :] = piece


def mix_kernel(blocks, *refs):
    slab_refs, wf_ref, top_ref, bottom_ref = refs[:blocks], *refs[blocks:]
    mix_part(slab_refs, wf_ref, ((top_ref, 0, HALO), (bottom_ref, HALO, HALO)))


def plane_pair(p, pieces):
    return jnp.concatenate([jnp.concatenate([piece(q) for piece in pieces], 0) for q in (p, p + 1)], 1)


def whole(ref):
    return lambda q: ref[q]


def ratio_kernel(blocks, meta_ref, *refs):
    slab_refs = refs[:blocks]
    (
        wf_ref, top_ref, bottom_ref, above_ref, below_ref, measured_ref, yf_ref, xf_ref,
        out_top_ref, out_inner_ref, out_bottom_ref, inner_ref, rows_ref,
    ) = refs[blocks:]
    planes, inner, width = inner_ref.shape
    rows = inner + 2 * HALO
    mix_part(slab_refs, wf_ref, ((inner_ref, 0, inner),))
    depth = (meta_ref.shape[0] - 2) // 2
    base = 2 + depth + meta_ref[0] * planes
    band = yf_ref[...]
    pieces = [whole(ref) for ref in (above_ref, top_ref, inner_ref, bottom_ref, below_ref)]
    for p in range(0, planes, 2):
        pair = halves(dot(band, split(plane_pair(p, pieces), 0)), 0)
        rows_ref[p] = pair[:, :width]
        rows_ref[p + 1] = pair[:, width:]
    circle = xf_ref[...]
    for p in range(0, planes, 4):
        four = rows_ref[p : p + 4].reshape(4 * rows, width)
        four = halves(dot(split(four, 1), circle), 1)
        for q in range(4):
            shift = meta_ref[base + p + q]
            forward = pltpu.roll(four[q * rows : (q + 1) * rows], shift, 1)
            inverse = pl.reciprocal(forward, approx=True)
            for _ in range(2):
                inverse = inverse * (2.0 - forward * inverse)
            ratio = measured_ref[0, p + q] * inverse
            ratio = pltpu.roll(ratio, lax.rem(width - shift, width), 1)
            out_top_ref[p + q] = ratio[:HALO]
            out_inner_ref[p + q] = ratio[HALO : rows - HALO]
            out_bottom_ref[p + q] = ratio[rows - HALO :]


def pull_part(rows_ref, xb_ref, wb_ref, out_refs):
    planes, part_rows, width = rows_ref.shape
    cells = planes * 8
    half = width // 2
    circle = xb_ref[...]
    for g in range(0, part_rows // 8, 2):
        cell = jnp.concatenate(
            [rows_ref[:, h * 8 : h * 8 + 8, :].reshape(cells, width) for h in (g, g + 1)], 0
        )
        turned = halves(dot(circle, split(cell, 1), 1), 0)
        turned = split(jnp.concatenate([turned[:, :cells], turned[:, cells:]], 0), 1)
        for d in range(len(out_refs) // 2):
            part = halves(dot(turned, wb_ref[d]), 1)
            for h in (0, 1):
                for e in (0, 1):
                    at = h * width + e * half
                    out_refs[2 * d + e][g + h] = part[at : at + half]


def pull_inner_kernel(top_ref, inner_ref, bottom_ref, yi_ref, xb_ref, wb_ref, *refs):
    out_refs, rows_ref = refs[:-1], refs[-1]
    planes, _, width = inner_ref.shape
    band = yi_ref[...]
    pieces = [whole(ref) for ref in (top_ref, inner_ref, bottom_ref)]
    for p in range(0, planes, 2):
        pair = halves(dot(band, split(plane_pair(p, pieces), 0)), 0)
        rows_ref[p] = pair[:, :width]
        rows_ref[p + 1] = pair[:, width:]
    pull_part(rows_ref, xb_ref, wb_ref, out_refs)


def pull_edge_kernel(top_ref, inner_ref, bottom_ref, above_ref, below_ref, ye_ref, xb_ref, wb_ref, *refs):
    out_refs, rows_ref = refs[:-1], refs[-1]
    planes, inner, width = inner_ref.shape
    band = ye_ref[...]
    for at, pieces in (
        (0, (whole(above_ref), whole(top_ref), lambda q: inner_ref[q, :HALO])),
        (HALO, (lambda q: inner_ref[q, inner - HALO :], whole(bottom_ref), whole(below_ref))),
    ):
        for p in range(0, planes, 2):
            pair = halves(dot(band, split(plane_pair(p, pieces), 0)), 0)
            rows_ref[p, at : at + HALO] = pair[:, :width]
            rows_ref[p + 1, at : at + HALO] = pair[:, width:]
    pull_part(rows_ref, xb_ref, wb_ref, out_refs)


def gather_kernel(blocks, views, meta_ref, *refs):
    part_refs, out_refs = refs[:blocks], refs[blocks:]
    share = out_refs[0].shape[1]
    for k, out_ref in enumerate(out_refs):
        start = pl.multiple_of(lax.rem(meta_ref[1] // 2 + k, views // 2) * share, share)
        total = part_refs[0][:, pl.ds(start, share), :]
        for ref in part_refs[1:]:
            total = total + ref[:, pl.ds(start, share), :]
        out_ref[...] = total


def update_kernel(count, old_edge_ref, old_inner_ref, *refs):
    edge_refs, inner_refs, out_ref = refs[:count], refs[count : 2 * count], refs[2 * count]
    planes, share, rows = out_ref.shape

    def products(old_ref, share_refs):
        blocks = []
        for g in range(old_ref.shape[0]):
            total = share_refs[0][g]
            for ref in share_refs[1:]:
                total = total + ref[g]
            blocks.append(total * old_ref[g])
        return blocks

    edge = products(old_edge_ref, edge_refs)
    middle = len(edge) // 2
    blocks = edge[:middle] + products(old_inner_ref, inner_refs) + edge[middle:]
    count_blocks = len(blocks)
    lane_block = iota((share, planes * 8), 1) // 8
    step = 1
    while step < count_blocks:
        low = (lane_block & step) == 0
        for g in range(count_blocks):
            if not g & step:
                a, b = blocks[g], blocks[g + step]
                blocks[g] = jnp.where(low, a, pltpu.roll(b, 8 * step, 1))
                blocks[g + step] = jnp.where(low, pltpu.roll(a, planes * 8 - 8 * step, 1), b)
        step *= 2
    for z in range(planes):
        at = (z // count_blocks) * rows
        out_ref[z] = blocks[z % count_blocks][:, at : at + rows]


def call(kernel, outs, specs, flops, name, scratch=()):
    spaces = {"s": pltpu.SMEM, "v": pltpu.VMEM}
    vmem = pl.BlockSpec(memory_space=pltpu.VMEM)
    single = not isinstance(outs, (list, tuple))
    return pl.pallas_call(
        kernel,
        out_shape=outs,
        in_specs=[pl.BlockSpec(memory_space=spaces[s]) for s in specs],
        out_specs=vmem if single else [vmem] * len(outs),
        scratch_shapes=list(scratch),
        compiler_params=pltpu.CompilerParams(vmem_limit_bytes=VMEM_LIMIT),
        cost_estimate=pl.CostEstimate(flops=flops, bytes_accessed=1 << 20, transcendentals=0),
        name=name,
    )


def local(estimate, measured, psf_taps, plane_source, plane_shift):
    planes, rows, width = estimate.shape
    devices = lax.axis_size("slab")
    tiles = lax.axis_size("tile")
    views = lax.axis_size("view")
    slab = lax.axis_index("slab")
    view = lax.axis_index("view")
    cells = planes * 8
    inner_rows = rows - 2 * HALO
    share = width // views

    def cells_of(*shape):
        return jax.ShapeDtypeStruct(shape, F32)

    def matrix(*shape):
        return jax.ShapeDtypeStruct(shape, BF16)

    edge = cells_of(planes, HALO, width)
    edges = cells_of(planes, 2 * HALO, width)
    inner = cells_of(planes, inner_rows, width)
    edge_pairs = cells_of(2 * HALO // 8, width // 2, cells)
    inner_pairs = cells_of(inner_rows // 8, width // 2, cells)
    edge_shares = cells_of(2 * HALO // 8, share, cells)
    inner_shares = cells_of(inner_rows // 8, share, cells)

    def exchange_rows(top, bottom):
        above = lax.ppermute(bottom, "tile", [(i, (i + 1) % tiles) for i in range(tiles)])
        below = lax.ppermute(top, "tile", [((i + 1) % tiles, i) for i in range(tiles)])
        return above, below

    def all_slabs(part):
        return [part] + [
            lax.ppermute(part, "slab", [(i, (i + d) % devices) for i in range(devices)])
            for d in range(1, devices)
        ]

    def to_pairs(parts):
        return [parts[0]] + [
            lax.ppermute(
                parts[2 * d + e],
                ("slab", "view"),
                [
                    (i * views + v, (i - d) % devices * views + (v ^ e))
                    for i in range(devices)
                    for v in range(views)
                ],
            )
            for d, e in [(d, e) for d in range(1, devices) for e in (0, 1)] + [(0, 1)]
        ]

    def to_views(parts):
        return [parts[0]] + [
            lax.ppermute(parts[k], "view", [(i, (i + 2 * k) % views) for i in range(views)])
            for k in range(1, views // 2)
        ]

    own_edge = jnp.concatenate([estimate[:, :HALO], estimate[:, rows - HALO :]], 1)
    own_inner = estimate[:, HALO : rows - HALO]
    edge_slabs = all_slabs(own_edge)
    kernels = psf_taps[0] / jnp.sum(psf_taps[0], axis=1, keepdims=True)
    meta = jnp.concatenate([jnp.stack([slab, view]).astype(jnp.int32), plane_source[0], plane_shift[0]])
    wf, yf, xf = call(
        functools.partial(prepare_forward_kernel, devices),
        [
            matrix(devices, 2 * cells, 2 * cells),
            matrix(2 * rows, 2 * (rows + 2 * HALO)),
            matrix(2 * width, 2 * width),
        ],
        "ssv",
        1 << 26,
        "prepare_forward",
    )(kernels, meta, own_inner)
    wb, yi, ye, xb, old_edge, old_inner, own_inner = call(
        functools.partial(prepare_back_kernel, devices, views),
        [
            matrix(devices, 2 * cells, 2 * cells),
            matrix(2 * inner_rows, 2 * rows),
            matrix(2 * HALO, 6 * HALO),
            matrix(2 * width, 2 * width),
            edge_shares,
            inner_shares,
            inner,
        ],
        "ssvvv",
        1 << 26,
        "prepare_back",
        [pltpu.VMEM((width, cells), F32)],
    )(kernels, meta, own_edge, own_inner, yf)
    inner_slabs = all_slabs(own_inner)

    top, bottom = call(
        functools.partial(mix_kernel, devices), [edge, edge], "v" * (devices + 1), 1 << 26, "mix_edge"
    )(*edge_slabs, wf)
    above, below = exchange_rows(top, bottom)
    top, middle, bottom = call(
        functools.partial(ratio_kernel, devices),
        [edge, inner, edge],
        "s" + "v" * (devices + 8),
        1 << 28,
        "ratio",
        [pltpu.VMEM((planes, inner_rows, width), F32), pltpu.VMEM((planes, rows, width), F32)],
    )(meta, *inner_slabs, wf, top, bottom, above, below, measured, yf, xf)
    above, below = exchange_rows(top, bottom)
    inner_parts = call(
        pull_inner_kernel,
        [inner_pairs] * (2 * devices),
        "v" * 6,
        1 << 26,
        "pull_inner",
        [pltpu.VMEM((planes, inner_rows, width), F32)],
    )(top, middle, bottom, yi, xb, wb)
    inner_parts = to_pairs(inner_parts)
    edge_parts = call(
        pull_edge_kernel,
        [edge_pairs] * (2 * devices),
        "v" * 8,
        1 << 26,
        "pull_edge",
        [pltpu.VMEM((planes, 2 * HALO, width), F32)],
    )(top, middle, bottom, above, below, ye, xb, wb)
    edge_parts = to_pairs(edge_parts)

    def gathered(parts, shape, name):
        return to_views(
            call(
                functools.partial(gather_kernel, 2 * devices, views),
                [shape] * (views // 2),
                "s" + "v" * (2 * devices),
                1 << 24,
                name,
            )(meta, *parts)
        )

    inner_sums = gathered(inner_parts, inner_shares, "gather_inner")
    edge_sums = gathered(edge_parts, edge_shares, "gather_edge")
    turned = call(
        functools.partial(update_kernel, views // 2),
        cells_of(planes, share, rows),
        "v" * (2 + views),
        1 << 20,
        "update",
    )(old_edge, old_inner, *edge_sums, *inner_sums)
    return jnp.swapaxes(turned, 1, 2)


def solution(mesh):
    in_specs = (
        P("slab", "tile", None),
        P("view", "slab", "tile", None),
        P("view", None, None),
        P("view", None),
        P("view", None),
    )
    out_specs = P("slab", "tile", "view")
    return jax.shard_map(local, mesh=mesh, in_specs=in_specs, out_specs=out_specs, check_vma=False)
```

```python
import functools

import jax
import jax.numpy as jnp
from jax import lax
from jax.experimental import pallas as pl
from jax.experimental.pallas import tpu as pltpu
from jax.sharding import PartitionSpec as P

F32 = jnp.float32
BF16 = jnp.bfloat16
HALO = 16
VMEM_LIMIT = 40 * 1024 * 1024


def split(x, axis):
    high = x.astype(BF16)
    low = (x - high.astype(F32)).astype(BF16)
    return jnp.concatenate([high, low], axis)


def dot(a, b, b_axis=0):
    return lax.dot_general(a, b, (((1,), (b_axis,)), ((), ())), preferred_element_type=F32)


def halves(x, axis):
    middle = x.shape[axis] // 2
    return lax.slice_in_dim(x, 0, middle, axis=axis) + lax.slice_in_dim(x, middle, 2 * middle, axis=axis)


def iota(shape, axis):
    return lax.broadcasted_iota(jnp.int32, shape, axis)


def wrapped(offset, length):
    offset = jnp.where(offset < 0, offset + length, offset)
    return jnp.where(offset >= length, offset - length, offset)


def by_taps(offset, taps_ref, axis):
    out = jnp.zeros(offset.shape, F32)
    for t in range(taps_ref.shape[1]):
        out = jnp.where(offset == t, taps_ref[axis, t], out)
    return out


def left_pack(full):
    high = full.astype(BF16)
    low = (full - high.astype(F32)).astype(BF16)
    return jnp.concatenate(
        [jnp.concatenate([high, high], 1), jnp.concatenate([low, jnp.zeros_like(low)], 1)], 0
    )


def right_pack(full):
    high = full.astype(BF16)
    low = (full - high.astype(F32)).astype(BF16)
    return jnp.concatenate(
        [jnp.concatenate([high, low], 1), jnp.concatenate([high, jnp.zeros_like(low)], 1)], 0
    )


def row_band(taps_ref, out_rows, in_rows, lead, back):
    row = iota((out_rows, 2 * in_rows), 0)
    col = iota((out_rows, 2 * in_rows), 1)
    first = col < in_rows
    col = jnp.where(first, col, col - in_rows)
    full = by_taps(row - col + lead if back else col - row - lead, taps_ref, 1)
    high = full.astype(BF16)
    low = jnp.where(first, full - high.astype(F32), 0.0).astype(BF16)
    return jnp.concatenate([high, low], 0)


def plane_maps(devices, planes, meta_ref):
    own = meta_ref[0]
    cells = planes * 8
    row = iota((cells, cells), 0)
    col = iota((cells, cells), 1)
    source_row = jnp.zeros((cells, cells), jnp.int32)
    for p in range(planes):
        source_row = jnp.where((row >> 3) == p, meta_ref[2 + own * planes + p], source_row)
    return col >> 3, (row & 7) == (col & 7), source_row


def prepare_forward_kernel(devices, taps_ref, meta_ref, inner_ref, wf_ref, yf_ref, xf_ref):
    planes, inner, width = inner_ref.shape
    rows = inner + 2 * HALO
    own = meta_ref[0]
    radius = (taps_ref.shape[1] - 1) // 2
    col_plane, diagonal, source_row = plane_maps(devices, planes, meta_ref)

    def block(d, carry):
        first = lax.rem(own - d + devices, devices) * planes + radius
        offset = wrapped(first + col_plane - source_row, devices * planes)
        wf_ref[d] = left_pack(jnp.where(diagonal, by_taps(offset, taps_ref, 0), 0.0))
        return carry

    lax.fori_loop(0, devices, block, 0)
    yf_ref[...] = row_band(taps_ref, rows, rows + 2 * HALO, HALO - radius, False)
    offset = iota((width, width), 0) - iota((width, width), 1) + radius
    xf_ref[...] = right_pack(by_taps(wrapped(offset, width), taps_ref, 2))


def prepare_back_kernel(
    devices, views, taps_ref, meta_ref, edge_ref, inner_ref, _,
    wb_ref, yi_ref, ye_ref, xb_ref, old_edge_ref, old_inner_ref, inner_out_ref, turned_ref,
):
    planes, inner, width = inner_ref.shape
    inner_out_ref[...] = inner_ref[...]
    rows = inner + 2 * HALO
    own, view = meta_ref[0], meta_ref[1]
    radius = (taps_ref.shape[1] - 1) // 2
    col_plane, diagonal, source_row = plane_maps(devices, planes, meta_ref)

    def block(d, carry):
        first = lax.rem(own - d + devices, devices) * planes + radius
        offset = wrapped(first + col_plane - source_row, devices * planes)
        wb_ref[d] = right_pack(jnp.where(diagonal, by_taps(offset, taps_ref, 0), 0.0))
        return carry

    lax.fori_loop(0, devices, block, 0)
    yi_ref[...] = row_band(taps_ref, inner, rows, HALO + radius, True)
    ye_ref[...] = row_band(taps_ref, HALO, 3 * HALO, HALO + radius, True)
    share = width // views
    row = iota((width, width), 0)
    half = row // (width // 2)
    parity = (view & 1) ^ half
    column = (parity + 2 * ((row - half * (width // 2)) // share)) * share + row % share
    offset = column - iota((width, width), 1) + radius
    xb_ref[...] = left_pack(by_taps(wrapped(offset, width), taps_ref, 2))
    mine = pl.ds(pl.multiple_of(view * share, share), share)
    for part_ref, old_ref in ((edge_ref, old_edge_ref), (inner_ref, old_inner_ref)):
        for g in range(part_ref.shape[1] // 8):
            turned_ref[...] = part_ref[:, g * 8 : g * 8 + 8, :].reshape(planes * 8, width).T
            old_ref[g] = turned_ref[mine, :] * (1.0 / views)


def mix_part(slab_refs, first, wf_ref, xf_ref, own_ref, out_refs):
    planes, part_rows, width = slab_refs[0].shape
    cells = planes * 8
    circle = xf_ref[...]
    for start in range(0, part_rows, 16):
        total = None
        for d, ref in enumerate(slab_refs, first):
            cell = jnp.concatenate(
                [ref[:, start + s : start + s + 8, :].reshape(cells, width) for s in (0, 8)], 1
            )
            part = dot(wf_ref[d], split(cell, 0))
            total = part if total is None else total + part
        total = halves(total, 0)
        total = jnp.concatenate([total[:, :width], total[:, width:]], 0)
        total = halves(dot(split(total, 1), circle), 1)
        for s in (0, 8):
            piece = total[(s // 8) * cells : (s // 8 + 1) * cells].reshape(planes, 8, width)
            if own_ref is not None:
                piece = piece + own_ref[:, start + s : start + s + 8, :]
            for ref, at, size in out_refs:
                if at <= start + s < at + size:
                    ref[:, start + s - at : start + s - at + 8, :] = piece


def own_kernel(edge_ref, inner_ref, wf_ref, xf_ref, own_edge_ref, own_inner_ref):
    for ref, out_ref in ((edge_ref, own_edge_ref), (inner_ref, own_inner_ref)):
        mix_part([ref], 0, wf_ref, xf_ref, None, ((out_ref, 0, ref.shape[1]),))


def mix_kernel(others, *refs):
    slab_refs, (own_ref, wf_ref, xf_ref, top_ref, bottom_ref) = refs[:others], refs[others:]
    mix_part(slab_refs, 1, wf_ref, xf_ref, own_ref, ((top_ref, 0, HALO), (bottom_ref, HALO, HALO)))


def plane_pair(p, pieces):
    return jnp.concatenate([jnp.concatenate([piece(q) for piece in pieces], 0) for q in (p, p + 1)], 1)


def whole(ref):
    return lambda q: ref[q]


def ratio_kernel(others, meta_ref, *refs):
    slab_refs = refs[:others]
    (
        own_ref, wf_ref, xf_ref, top_ref, bottom_ref, above_ref, below_ref, measured_ref, yf_ref,
        out_top_ref, out_inner_ref, out_bottom_ref, inner_ref,
    ) = refs[others:]
    planes, inner, width = inner_ref.shape
    rows = inner + 2 * HALO
    mix_part(slab_refs, 1, wf_ref, xf_ref, own_ref, ((inner_ref, 0, inner),))
    depth = (meta_ref.shape[0] - 2) // 2
    base = 2 + depth + meta_ref[0] * planes
    band = yf_ref[...]
    pieces = [whole(ref) for ref in (above_ref, top_ref, inner_ref, bottom_ref, below_ref)]
    for p in range(0, planes, 2):
        pair = halves(dot(band, split(plane_pair(p, pieces), 0)), 0)
        for q in (0, 1):
            shift = meta_ref[base + p + q]
            forward = pltpu.roll(pair[:, q * width : (q + 1) * width], shift, 1)
            inverse = pl.reciprocal(forward, approx=True)
            for _ in range(2):
                inverse = inverse * (2.0 - forward * inverse)
            ratio = measured_ref[0, p + q] * inverse
            ratio = pltpu.roll(ratio, lax.rem(width - shift, width), 1)
            out_top_ref[p + q] = ratio[:HALO]
            out_inner_ref[p + q] = ratio[HALO : rows - HALO]
            out_bottom_ref[p + q] = ratio[rows - HALO :]


def pull_part(rows_ref, xb_ref, wb_ref, out_refs):
    planes, part_rows, width = rows_ref.shape
    cells = planes * 8
    half = width // 2
    circle = xb_ref[...]
    for g in range(0, part_rows // 8, 2):
        cell = jnp.concatenate(
            [rows_ref[:, h * 8 : h * 8 + 8, :].reshape(cells, width) for h in (g, g + 1)], 0
        )
        turned = halves(dot(circle, split(cell, 1), 1), 0)
        turned = split(jnp.concatenate([turned[:, :cells], turned[:, cells:]], 0), 1)
        for d in range(len(out_refs) // 2):
            part = halves(dot(turned, wb_ref[d]), 1)
            for h in (0, 1):
                for e in (0, 1):
                    at = h * width + e * half
                    out_refs[2 * d + e][g + h] = part[at : at + half]


def pull_inner_kernel(top_ref, inner_ref, bottom_ref, yi_ref, xb_ref, wb_ref, *refs):
    out_refs, rows_ref = refs[:-1], refs[-1]
    planes, _, width = inner_ref.shape
    band = yi_ref[...]
    pieces = [whole(ref) for ref in (top_ref, inner_ref, bottom_ref)]
    for p in range(0, planes, 2):
        pair = halves(dot(band, split(plane_pair(p, pieces), 0)), 0)
        rows_ref[p] = pair[:, :width]
        rows_ref[p + 1] = pair[:, width:]
    pull_part(rows_ref, xb_ref, wb_ref, out_refs)


def pull_edge_kernel(top_ref, inner_ref, bottom_ref, above_ref, below_ref, ye_ref, xb_ref, wb_ref, *refs):
    out_refs, rows_ref = refs[:-1], refs[-1]
    planes, inner, width = inner_ref.shape
    band = ye_ref[...]
    for at, pieces in (
        (0, (whole(above_ref), whole(top_ref), lambda q: inner_ref[q, :HALO])),
        (HALO, (lambda q: inner_ref[q, inner - HALO :], whole(bottom_ref), whole(below_ref))),
    ):
        for p in range(0, planes, 2):
            pair = halves(dot(band, split(plane_pair(p, pieces), 0)), 0)
            rows_ref[p, at : at + HALO] = pair[:, :width]
            rows_ref[p + 1, at : at + HALO] = pair[:, width:]
    pull_part(rows_ref, xb_ref, wb_ref, out_refs)


def gather_kernel(blocks, views, meta_ref, *refs):
    part_refs, out_refs = refs[:blocks], refs[blocks:]
    share = out_refs[0].shape[1]
    for k, out_ref in enumerate(out_refs):
        start = pl.multiple_of(lax.rem(meta_ref[1] // 2 + k, views // 2) * share, share)
        total = part_refs[0][:, pl.ds(start, share), :]
        for ref in part_refs[1:]:
            total = total + ref[:, pl.ds(start, share), :]
        out_ref[...] = total


def update_kernel(count, old_edge_ref, old_inner_ref, *refs):
    edge_refs, inner_refs, out_ref = refs[:count], refs[count : 2 * count], refs[2 * count]
    planes, share, rows = out_ref.shape

    def products(old_ref, share_refs):
        blocks = []
        for g in range(old_ref.shape[0]):
            total = share_refs[0][g]
            for ref in share_refs[1:]:
                total = total + ref[g]
            blocks.append(total * old_ref[g])
        return blocks

    edge = products(old_edge_ref, edge_refs)
    middle = len(edge) // 2
    blocks = edge[:middle] + products(old_inner_ref, inner_refs) + edge[middle:]
    count_blocks = len(blocks)
    lane_block = iota((share, planes * 8), 1) // 8
    step = 1
    while step < count_blocks:
        low = (lane_block & step) == 0
        for g in range(count_blocks):
            if not g & step:
                a, b = blocks[g], blocks[g + step]
                blocks[g] = jnp.where(low, a, pltpu.roll(b, 8 * step, 1))
                blocks[g + step] = jnp.where(low, pltpu.roll(a, planes * 8 - 8 * step, 1), b)
        step *= 2
    for z in range(planes):
        at = (z // count_blocks) * rows
        out_ref[z] = blocks[z % count_blocks][:, at : at + rows]


def call(kernel, outs, specs, flops, name, scratch=()):
    spaces = {"s": pltpu.SMEM, "v": pltpu.VMEM}
    vmem = pl.BlockSpec(memory_space=pltpu.VMEM)
    single = not isinstance(outs, (list, tuple))
    return pl.pallas_call(
        kernel,
        out_shape=outs,
        in_specs=[pl.BlockSpec(memory_space=spaces[s]) for s in specs],
        out_specs=vmem if single else [vmem] * len(outs),
        scratch_shapes=list(scratch),
        compiler_params=pltpu.CompilerParams(vmem_limit_bytes=VMEM_LIMIT),
        cost_estimate=pl.CostEstimate(flops=flops, bytes_accessed=1 << 20, transcendentals=0),
        name=name,
    )


def local(estimate, measured, psf_taps, plane_source, plane_shift):
    planes, rows, width = estimate.shape
    devices = lax.axis_size("slab")
    tiles = lax.axis_size("tile")
    views = lax.axis_size("view")
    slab = lax.axis_index("slab")
    view = lax.axis_index("view")
    cells = planes * 8
    inner_rows = rows - 2 * HALO
    share = width // views

    def cells_of(*shape):
        return jax.ShapeDtypeStruct(shape, F32)

    def matrix(*shape):
        return jax.ShapeDtypeStruct(shape, BF16)

    edge = cells_of(planes, HALO, width)
    edges = cells_of(planes, 2 * HALO, width)
    inner = cells_of(planes, inner_rows, width)
    edge_pairs = cells_of(2 * HALO // 8, width // 2, cells)
    inner_pairs = cells_of(inner_rows // 8, width // 2, cells)
    edge_shares = cells_of(2 * HALO // 8, share, cells)
    inner_shares = cells_of(inner_rows // 8, share, cells)

    def exchange_rows(top, bottom):
        above = lax.ppermute(bottom, "tile", [(i, (i + 1) % tiles) for i in range(tiles)])
        below = lax.ppermute(top, "tile", [((i + 1) % tiles, i) for i in range(tiles)])
        return above, below

    def all_slabs(part):
        return [part] + [
            lax.ppermute(part, "slab", [(i, (i + d) % devices) for i in range(devices)])
            for d in range(1, devices)
        ]

    def to_pairs(parts):
        return [parts[0]] + [
            lax.ppermute(
                parts[2 * d + e],
                ("slab", "view"),
                [
                    (i * views + v, (i - d) % devices * views + (v ^ e))
                    for i in range(devices)
                    for v in range(views)
                ],
            )
            for d, e in [(d, e) for d in range(1, devices) for e in (0, 1)] + [(0, 1)]
        ]

    def to_views(parts):
        return [parts[0]] + [
            lax.ppermute(parts[k], "view", [(i, (i + 2 * k) % views) for i in range(views)])
            for k in range(1, views // 2)
        ]

    own_edge = jnp.concatenate([estimate[:, :HALO], estimate[:, rows - HALO :]], 1)
    own_inner = estimate[:, HALO : rows - HALO]
    edge_slabs = all_slabs(own_edge)
    kernels = psf_taps[0] / jnp.sum(psf_taps[0], axis=1, keepdims=True)
    meta = jnp.concatenate([jnp.stack([slab, view]).astype(jnp.int32), plane_source[0], plane_shift[0]])
    wf, yf, xf = call(
        functools.partial(prepare_forward_kernel, devices),
        [
            matrix(devices, 2 * cells, 2 * cells),
            matrix(2 * rows, 2 * (rows + 2 * HALO)),
            matrix(2 * width, 2 * width),
        ],
        "ssv",
        1 << 26,
        "prepare_forward",
    )(kernels, meta, own_inner)
    own_edge_part, own_inner_part = call(own_kernel, [edges, inner], "vvvv", 1 << 26, "own")(
        own_edge, own_inner, wf, xf
    )
    wb, yi, ye, xb, old_edge, old_inner, own_inner = call(
        functools.partial(prepare_back_kernel, devices, views),
        [
            matrix(devices, 2 * cells, 2 * cells),
            matrix(2 * inner_rows, 2 * rows),
            matrix(2 * HALO, 6 * HALO),
            matrix(2 * width, 2 * width),
            edge_shares,
            inner_shares,
            inner,
        ],
        "ssvvv",
        1 << 26,
        "prepare_back",
        [pltpu.VMEM((width, cells), F32)],
    )(kernels, meta, own_edge, own_inner, own_edge_part)
    inner_slabs = all_slabs(own_inner)

    top, bottom = call(
        functools.partial(mix_kernel, devices - 1), [edge, edge], "v" * (devices + 2), 1 << 26, "mix_edge"
    )(*edge_slabs[1:], own_edge_part, wf, xf)
    above, below = exchange_rows(top, bottom)
    top, middle, bottom = call(
        functools.partial(ratio_kernel, devices - 1),
        [edge, inner, edge],
        "s" + "v" * (devices + 8),
        1 << 28,
        "ratio",
        [pltpu.VMEM((planes, inner_rows, width), F32)],
    )(meta, *inner_slabs[1:], own_inner_part, wf, xf, top, bottom, above, below, measured, yf)
    above, below = exchange_rows(top, bottom)
    inner_parts = call(
        pull_inner_kernel,
        [inner_pairs] * (2 * devices),
        "v" * 6,
        1 << 26,
        "pull_inner",
        [pltpu.VMEM((planes, inner_rows, width), F32)],
    )(top, middle, bottom, yi, xb, wb)
    inner_parts = to_pairs(inner_parts)
    edge_parts = call(
        pull_edge_kernel,
        [edge_pairs] * (2 * devices),
        "v" * 8,
        1 << 26,
        "pull_edge",
        [pltpu.VMEM((planes, 2 * HALO, width), F32)],
    )(top, middle, bottom, above, below, ye, xb, wb)
    edge_parts = to_pairs(edge_parts)

    def gathered(parts, shape, name):
        return to_views(
            call(
                functools.partial(gather_kernel, 2 * devices, views),
                [shape] * (views // 2),
                "s" + "v" * (2 * devices),
                1 << 24,
                name,
            )(meta, *parts)
        )

    inner_sums = gathered(inner_parts, inner_shares, "gather_inner")
    edge_sums = gathered(edge_parts, edge_shares, "gather_edge")
    turned = call(
        functools.partial(update_kernel, views // 2),
        cells_of(planes, share, rows),
        "v" * (2 + views),
        1 << 20,
        "update",
    )(old_edge, old_inner, *edge_sums, *inner_sums)
    return jnp.swapaxes(turned, 1, 2)


def solution(mesh):
    in_specs = (
        P("slab", "tile", None),
        P("view", "slab", "tile", None),
        P("view", None, None),
        P("view", None),
        P("view", None),
    )
    out_specs = P("slab", "tile", "view")
    return jax.shard_map(local, mesh=mesh, in_specs=in_specs, out_specs=out_specs, check_vma=False)
```
